128 devices in a mesh: rows: 16 (over z_lo, y, core), cols: 8 (over z_hi, x).
Axes of the slice: x: 4, y: 4, z: 4 (z_hi: 2, z_lo: 2; z = z_hi * 2 + z_lo), core: 2. Of those that a mesh axis runs over, the one named last changes fastest.
Arguments:
- features: bfloat16 [256, 768, 512], P('rows', 'cols'), may hold values from -6 to 6
- conv_taps: float32 [9, 512], replicated, may hold values from -2 to 2
- block_gain: float32 [512], replicated, may hold values from 0.1 to 1.9
- block_qkv: bfloat16 [512, 1536], replicated, may hold values from -1.3258252 to 1.3258252
- block_out: bfloat16 [512, 512], replicated, may hold values from -0.25 to 0.25
- grid_gain: float32 [512], replicated, may hold values from 0.1 to 1.9
- grid_qkv: bfloat16 [512, 1536], replicated, may hold values from -1.3258252 to 1.3258252
- grid_out: bfloat16 [512, 512], replicated, may hold values from -0.25 to 0.25
Outputs:
- encoded: bfloat16 [256, 768, 512], P('rows', 'cols')
The draws below stay inside these ranges and needn't reach their ends.
All inputs are finite; a program needn't handle non-finite values.
Results may differ from the reference program's by a relative error of at most 0.009.
Values may be sent and summed in bfloat16 or wider, within the bound.
A program may use at most 128 MiB of HBM per device.

```python
import jax
import jax.numpy as jnp
from jax import lax

D = 512
HEADS = 16
HEAD_DIM = 32
BLOCK = 8
GRID = 8
FRAME_ROWS = 256
FRAME_COLS = 768


def aligned_table(key, chosen):
    base = jnp.clip(jax.random.normal(key, (D, 3 * D), jnp.float32), -6.0, 6.0) * D ** (-0.5)
    column = jnp.arange(3 * D) % D
    head_of = column // HEAD_DIM
    selected = (head_of < chosen)[None, :]
    queries_part = base[:, :D]
    head_sel = selected[:, :D]
    new_queries = jnp.where(head_sel, queries_part, queries_part)
    new_keys = jnp.where(head_sel, queries_part, base[:, D:2 * D])
    return jnp.concatenate([new_queries, new_keys, base[:, 2 * D:]], axis=1)


def draw_block_qkv(key, part):
    key = jax.random.fold_in(key, 11)
    return aligned_table(key, 0).astype(jnp.bfloat16)


def draw_grid_qkv(key, part):
    key = jax.random.fold_in(key, 23)
    return aligned_table(key, 0).astype(jnp.bfloat16)


def levels(rng, extent, shards, least, top_value):
    level = 1.0
    for position, parts in shards:
        steps = jax.random.uniform(jax.random.fold_in(jax.random.fold_in(rng, 6), position), (parts,), jnp.float32, least / len(shards), top_value / len(shards))
        level = level * jnp.repeat(jnp.exp(steps), extent[position] // parts).reshape((-1,) + (1,) * (len(extent) - 1 - position))
    return level


def gaussian(own_key, dims, scale, bound, split=(), kind=jnp.bfloat16):
    drawn = jax.random.normal(own_key, dims, jnp.float32) * scale
    if len(split) > 0:
        drawn = levels(own_key, dims, split, -0.22, 0.18) * drawn
    return jnp.clip(drawn, min=-bound, max=bound).astype(kind)


def setup_inputs(seed: int = 0) -> dict:
    splits = jax.random.split(jax.random.key(seed), 9)
    return {
        "features": gaussian(splits[0], (FRAME_ROWS, FRAME_COLS, D), 1.0, 6.0, ((0, 16), (1, 8))),
        "conv_taps": gaussian(splits[1], (9, D), 0.35, 2.0, (), jnp.float32),
        "block_gain": jnp.clip(1.0 + 0.18 * jax.random.normal(splits[2], (D,), jnp.float32), 0.1, 1.9),
        "block_qkv": draw_block_qkv(jax.random.fold_in(splits[8], 71), 0),
        "block_out": gaussian(splits[4], (D, D), D ** -0.5, 0.25),
        "grid_gain": jnp.clip(1.0 + 0.18 * jax.random.normal(splits[5], (D,), jnp.float32), 0.1, 1.9),
        "grid_qkv": draw_grid_qkv(jax.random.fold_in(splits[8], 71), 0),
        "grid_out": gaussian(splits[7], (D, D), D ** -0.5, 0.25),
    }


def window_attention(windows, gain, w_qkv, w_out):
    count, length, channels = windows.shape
    head_dim = channels // HEADS
    wide = windows.astype(jnp.float32)
    average = lax.optimization_barrier(jnp.mean(wide, axis=-1, keepdims=True))
    centred = wide - average
    spread = lax.optimization_barrier(jnp.mean(centred * centred, axis=-1, keepdims=True))
    normed = (centred * lax.rsqrt(spread + 1e-05) * gain).astype(jnp.bfloat16)
    projected = jnp.dot(normed.reshape(count * length, channels), w_qkv, preferred_element_type=jnp.float32)
    projected = projected.astype(jnp.bfloat16).reshape(count, length, 3, HEADS, head_dim)
    queries = projected[:, :, 0].astype(jnp.float32)
    keys_all = projected[:, :, 1].astype(jnp.float32)
    values_all = projected[:, :, 2].astype(jnp.float32)
    scores = jnp.einsum('nqhe,nkhe->nhqk', queries, keys_all) * head_dim ** (-0.5)
    weights_soft = jax.nn.softmax(scores, axis=-1).astype(jnp.bfloat16)
    attended = jnp.einsum('nhqk,nkhe->nqhe', weights_soft.astype(jnp.float32), values_all).astype(jnp.bfloat16)
    output = jnp.dot(attended.reshape(count * length, channels), w_out, preferred_element_type=jnp.float32)
    return (output.reshape(count, length, channels) + wide).astype(jnp.bfloat16)

def reference(features, conv_taps, block_gain, block_qkv, block_out, grid_gain, grid_qkv, grid_out):
    total_rows, total_cols, channels = features.shape
    wide = features.astype(jnp.float32)
    padded = jnp.pad(wide, ((1, 1), (1, 1), (0, 0)))
    filtered = wide
    for tap_index in range(9):
        row_off = tap_index // 3
        col_off = tap_index % 3
        filtered = filtered + conv_taps[tap_index] * padded[row_off:row_off + total_rows, col_off:col_off + total_cols]
    convolved = filtered.astype(jnp.bfloat16)
    bands = convolved.reshape(total_rows // BLOCK, BLOCK, total_cols // BLOCK, BLOCK, channels)

    def block_band(band):
        windows = band.transpose(1, 0, 2, 3).reshape(total_cols // BLOCK, BLOCK * BLOCK, channels)
        result = window_attention(windows, block_gain, block_qkv, block_out)
        return result.reshape(total_cols // BLOCK, BLOCK, BLOCK, channels).transpose(1, 0, 2, 3)
    blocked = lax.map(block_band, bands).reshape(total_rows, total_cols, channels)
    spaced = blocked.reshape(GRID, total_rows // GRID, GRID, total_cols // GRID, channels).transpose(1, 0, 2, 3, 4)

    def grid_band(band):
        windows = band.transpose(2, 0, 1, 3).reshape(total_cols // GRID, GRID * GRID, channels)
        result = window_attention(windows, grid_gain, grid_qkv, grid_out)
        return result.reshape(total_cols // GRID, GRID, GRID, channels).transpose(1, 2, 0, 3)
    encoded = lax.map(grid_band, spaced).transpose(1, 0, 2, 3, 4)
    return encoded.reshape(total_rows, total_cols, channels)
```

```python
import jax
import jax.numpy as jnp
from jax import lax
from jax.experimental import pallas as pl
from jax.experimental.pallas import tpu as pltpu
from jax.sharding import PartitionSpec as P

MESH = pl.DeviceIdType.MESH
BF = jnp.bfloat16
F32 = jnp.float32
HEAD_DIM = 32
SCALE = HEAD_DIM ** -0.5
CHUNKS = 3
PEERS = 64
TOK = 512


def mm(a, b, dims=((1,), (0,))):
    return lax.dot_general(a, b, (dims, ((), ())), preferred_element_type=F32)


def norm_rows(x, gain):
    mean = jnp.mean(x, axis=-1, keepdims=True)
    cen = x - mean
    var = jnp.mean(cen * cen, axis=-1, keepdims=True)
    return (cen * lax.rsqrt(var + 1e-5) * gain).astype(BF)


def spread_heads(q):
    cols = []
    for h in range(4):
        parts = []
        if h > 0:
            parts.append(jnp.zeros((32 * h, 128), BF))
        parts.append(q[32 * h : 32 * (h + 1)])
        if h < 3:
            parts.append(jnp.zeros((32 * (3 - h), 128), BF))
        cols.append(jnp.concatenate(parts, axis=0))
    return jnp.concatenate(cols, axis=1)


def scores(unit, k_scr, qvt_scr):
    p, g = unit
    keys = k_scr[p * 128 : (p + 1) * 128, g * 128 : (g + 1) * 128]
    q = qvt_scr[g * 128 : (g + 1) * 128, p * 128 : (p + 1) * 128]
    s4 = mm(keys, spread_heads(q))
    first = lax.broadcasted_iota(jnp.int32, (64, 128), 1) < 64
    return [
        jnp.where(first, s4[:64, h * 128 : (h + 1) * 128], s4[64:, h * 128 : (h + 1) * 128])
        for h in range(4)
    ]


def soft(heads):
    lane = lax.broadcasted_iota(jnp.int32, (64, 128), 1)
    low = jnp.where(lane < 64, 1.0, 0.0).astype(BF)
    high = jnp.where(lane < 64, 0.0, 1.0).astype(BF)
    probs, inverse = [], []
    for s in heads:
        m = jnp.max(s, axis=0, keepdims=True)
        e = jnp.exp((s - m) * SCALE)
        inverse.append(1.0 / jnp.sum(e, axis=0, keepdims=True))
        pb = e.astype(BF)
        probs.append(jnp.concatenate([pb * low, pb * high], axis=0))
    return probs, inverse


def weigh(unit, softened, qvt_scr, ot_scr):
    p, g = unit
    probs, inverse = softened
    for h in range(0, 4, 2):
        r = g * 128 + h * 32
        v2 = qvt_scr[512 + r : 512 + r + 64, p * 128 : (p + 1) * 128]
        o2 = mm(v2, jnp.concatenate([probs[h], probs[h + 1]], axis=1))
        o = jnp.concatenate([o2[:32, :128] * inverse[h], o2[32:, 128:] * inverse[h + 1]], axis=0)
        ot_scr[r : r + 64, p * 128 : (p + 1) * 128] = o.astype(BF)


def attend(k_scr, qvt_scr, ot_scr):
    units = [(p, g) for p in range(4) for g in range(4)]
    n, b = len(units), 2
    ready = [scores(u, k_scr, qvt_scr) for u in units[:b]]
    last = None
    for i in range(0, n, b):
        now = ready
        if i + b < n:
            ready = [scores(u, k_scr, qvt_scr) for u in units[i + b : i + 2 * b]]
        done = [soft(s) for s in now]
        if last is not None:
            for u, x in zip(units[i - b : i], last):
                weigh(u, x, qvt_scr, ot_scr)
        last = done
    for u, x in zip(units[n - b :], last):
        weigh(u, x, qvt_scr, ot_scr)


def sublayer(n_scr, wk_scr, wqvt_scr, wo_scr, k_scr, qvt_scr, ot_scr):
    normed = n_scr[...]
    k_scr[...] = mm(normed, wk_scr[...]).astype(BF)
    qvt_scr[...] = mm(wqvt_scr[...], normed, ((1,), (1,))).astype(BF)
    attend(k_scr, qvt_scr, ot_scr)
    return mm(ot_scr[...], wo_scr[...], ((0,), (0,)))


def to_planes(x):
    y = x.reshape(PEERS, 8, 512)
    return jnp.concatenate([y[:, :, :256], y[:, :, 256:]], axis=1).astype(BF)


def from_planes(planes):
    y = planes.astype(F32)
    return jnp.concatenate([y[:, :8], y[:, 8:]], axis=2)


def main_kernel(
    feat_ref, taps_ref, bgain_ref, ggain_ref, bqkv_ref, bout_ref, gqkv_ref, gout_ref,
    ret_ref,
    fpad, coll, colr, lcol, rcol, x_scr, g_scr,
    bqkv, gqkv, bwo, gwo, wk_scr, wqvt_scr, n_scr, k_scr, qvt_scr, ot_scr,
    snd, rcv, snd2,
    local_sem, halo_send, halo_recv, ssem, rsem, ssem2, rsem2, own_sem,
):
    ri, ci = lax.axis_index("rows"), lax.axis_index("cols")
    core = lax.rem(ri, 2)
    me = (ri // 2) * 8 + ci
    up, down = lax.rem(ri + 15, 16), lax.rem(ri + 1, 16)
    left, right = lax.rem(ci + 7, 8), lax.rem(ci + 1, 8)

    load_feat = pltpu.make_async_copy(feat_ref, fpad.at[pl.ds(1, 16)], local_sem.at[0])
    load_feat.start()
    loads = [
        pltpu.make_async_copy(src, dst, local_sem.at[i + 1])
        for i, (src, dst) in enumerate(((bqkv_ref, bqkv), (bout_ref, bwo), (gqkv_ref, gqkv), (gout_ref, gwo)))
    ]
    for load in loads:
        load.start()

    def peer(d):
        t = lax.rem(me + d, PEERS)
        return t, (2 * (t // 8) + core, lax.rem(t, 8))

    barrier = pltpu.get_barrier_semaphore()

    def greet(d, carry):
        pl.semaphore_signal(barrier, inc=1, device_id=peer(d)[1], device_id_type=MESH)
        return carry

    around = [(r, c) for r in (up, down) for c in (left, ci, right)]
    for r, c in around:
        pl.semaphore_signal(barrier, inc=1, device_id=(r, c), device_id_type=MESH)
    lax.fori_loop(1, PEERS, greet, 0)

    load_feat.wait()
    for r in range(16):
        coll[r : r + 1, :] = fpad[r + 1, 0:1, :]
        colr[r : r + 1, :] = fpad[r + 1, 95:96, :]
    pl.semaphore_wait(barrier, PEERS - 1 + len(around))

    halo = [
        (fpad.at[1], fpad.at[17], (up, ci)),
        (fpad.at[16], fpad.at[0], (down, ci)),
        (coll, rcol.at[1], (ri, left)),
        (colr, lcol.at[1], (ri, right)),
        (coll, rcol.at[2], (up, left)),
        (coll, rcol.at[0], (down, left)),
        (colr, lcol.at[2], (up, right)),
        (colr, lcol.at[0], (down, right)),
    ]
    halo = [
        pltpu.make_async_remote_copy(
            src, dst, halo_send.at[i], halo_recv.at[i], device_id=to, device_id_type=MESH
        )
        for i, (src, dst, to) in enumerate(halo)
    ]
    for copy in halo:
        copy.start()

    def conv_row(r, above, below):
        half, rr = r // 8, lax.rem(r, 8)
        first = lax.broadcasted_iota(jnp.int32, (96, 128), 0) == 0
        last = lax.broadcasted_iota(jnp.int32, (96, 128), 0) == 95
        for lt in range(4):
            lanes = slice(lt * 128, (lt + 1) * 128)
            xm = fpad[r, :, lanes].astype(F32)
            x0 = fpad[r + 1, :, lanes].astype(F32)
            xp = fpad[r + 2, :, lanes].astype(F32)
            if above is not None:
                xm = jnp.where(above, xm, 0.0)
            if below is not None:
                xp = jnp.where(below, xp, 0.0)
            tap = [taps_ref[k : k + 1, lanes] for k in range(9)]
            a0 = tap[0] * xm + tap[3] * x0 + tap[6] * xp
            a1 = tap[1] * xm + tap[4] * x0 + tap[7] * xp
            a2 = tap[2] * xm + tap[5] * x0 + tap[8] * xp
            a0 = jnp.where(first, 0.0, pltpu.roll(a0, 1, 0))
            a2 = jnp.where(last, 0.0, pltpu.roll(a2, 95, 0))
            y = x0 + a1 + a0 + a2
            for t in range(CHUNKS):
                for j in range(4):
                    c = (4 * t + j) * 8
                    x_scr[t, half, j, rr, :, lanes] = y[c : c + 8]

    def inner(r, carry):
        conv_row(r, None, None)
        return carry

    lax.fori_loop(1, 15, inner, 0)

    def prepare(wqkv, load):
        load.wait()
        wk_scr[...] = wqkv[:, 512:1024]
        wqvt_scr[:512] = wqkv[:, :512].T
        wqvt_scr[512:] = wqkv[:, 1024:].T

    prepare(bqkv, loads[0])
    loads[1].wait()

    for copy in halo:
        copy.wait_recv()
    not_top, not_bottom = ri > 0, ri < 15
    conv_row(0, not_top, None)
    conv_row(15, None, not_bottom)
    row_of = lax.broadcasted_iota(jnp.int32, (16, 512), 0)
    sub = lax.broadcasted_iota(jnp.int32, (8, 512), 0)
    for cols, inside, k0, j, t, at in ((lcol, ci > 0, 0, 0, 0, 0), (rcol, ci < 7, 2, 3, 2, 7)):
        here = cols[1].astype(F32)
        before = jnp.where(not_top, cols[0].astype(F32)[15:16], 0.0)
        after = jnp.where(not_bottom, cols[2].astype(F32)[0:1], 0.0)
        shifted_m = jnp.where(row_of == 0, before, pltpu.roll(here, 1, 0))
        shifted_p = jnp.where(row_of == 15, after, pltpu.roll(here, 15, 0))
        edge = (
            taps_ref[k0 : k0 + 1, :] * shifted_m
            + taps_ref[k0 + 3 : k0 + 4, :] * here
            + taps_ref[k0 + 6 : k0 + 7, :] * shifted_p
        )
        edge = jnp.where(inside, edge, 0.0)
        for r in range(16):
            x_scr[t, r // 8, j, r % 8] += jnp.where(sub == at, edge[r : r + 1], 0.0)

    def send_all(t, src, dst, send, recv):
        def start(d, carry):
            slot, device = peer(d)
            pltpu.make_async_remote_copy(
                src.at[t, slot], dst.at[t, me], send.at[t], recv.at[t],
                device_id=device, device_id_type=MESH,
            ).start()
            return carry

        lax.fori_loop(1, PEERS, start, 0)

    def all_of(t, src, dst, send, recv):
        return pltpu.make_async_remote_copy(
            src.at[t, pl.ds(0, PEERS - 1)], dst.at[t, pl.ds(0, PEERS - 1)], send.at[t], recv.at[t],
            device_id=(ri, ci), device_id_type=MESH,
        )

    def block(t, carry):
        def rounded():
            return x_scr[t].reshape(TOK, 512).astype(BF).astype(F32)

        n_scr[...] = norm_rows(rounded(), bgain_ref[...])
        out = sublayer(n_scr, wk_scr, wqvt_scr, bwo, k_scr, qvt_scr, ot_scr)
        snd[t] = to_planes(out + rounded())
        rcv[t, me] = snd[t, me]
        send_all(t, snd, rcv, ssem, rsem)
        return carry

    lax.fori_loop(0, CHUNKS, block, 0)
    prepare(gqkv, loads[2])
    loads[3].wait()

    def grid(t, carry):
        all_of(t, snd, rcv, ssem, rsem).wait_recv()
        arrived = rcv[t].astype(F32)
        for lt in range(4):
            rows, lanes = slice(8 * (lt // 2), 8 * (lt // 2) + 8), slice(128 * (lt % 2), 128 * (lt % 2) + 128)
            g_scr[lt] = arrived[:, rows, lanes].reshape(TOK, 128)
        for q in range(8):
            window = jnp.concatenate([g_scr[lt, pl.ds(q, 64, stride=8), :] for lt in range(4)], axis=1)
            n_scr[q * 64 : (q + 1) * 64] = norm_rows(window, ggain_ref[...])
        out = sublayer(n_scr, wk_scr, wqvt_scr, gwo, k_scr, qvt_scr, ot_scr)
        for q in range(8):
            for lt in range(4):
                g_scr[lt, pl.ds(q, 64, stride=8), :] += out[q * 64 : (q + 1) * 64, lt * 128 : (lt + 1) * 128]
        snd2[t] = to_planes(jnp.concatenate([g_scr[lt] for lt in range(4)], axis=1))
        own = pltpu.make_async_copy(snd2.at[t, me], ret_ref.at[t, me], own_sem)
        own.start()
        send_all(t, snd2, ret_ref, ssem2, rsem2)
        own.wait()
        return carry

    lax.fori_loop(0, CHUNKS, grid, 0)

    for copy in halo:
        copy.wait_send()
    for t in range(CHUNKS):
        all_of(t, snd, rcv, ssem, rsem).wait_send()
    for t in range(CHUNKS):
        back = all_of(t, snd2, ret_ref, ssem2, rsem2)
        back.wait_send()
        back.wait_recv()


def unpack_kernel(ret_ref, out_ref):
    y = from_planes(ret_ref[0]).reshape(2, 4, 8, 8, 512)
    out_ref[...] = y.transpose(0, 2, 1, 3, 4).reshape(16, 32, 512).astype(BF)


def body(features, conv_taps, block_gain, block_qkv, block_out, grid_gain, grid_qkv, grid_out):
    any_ = pl.BlockSpec(memory_space=pl.ANY)
    vmem = pl.BlockSpec(memory_space=pltpu.VMEM)
    dma = pltpu.SemaphoreType.DMA
    planes = (CHUNKS, PEERS, 16, 256)
    returned = pl.pallas_call(
        main_kernel,
        out_shape=jax.ShapeDtypeStruct(planes, BF),
        in_specs=[any_, vmem, vmem, vmem, any_, any_, any_, any_],
        out_specs=any_,
        scratch_shapes=[
            pltpu.VMEM((18, 96, 512), BF),
            pltpu.VMEM((16, 512), BF),
            pltpu.VMEM((16, 512), BF),
            pltpu.VMEM((3, 16, 512), BF),
            pltpu.VMEM((3, 16, 512), BF),
            pltpu.VMEM((CHUNKS, 2, 4, 8, 8, 512), F32),
            pltpu.VMEM((4, TOK, 128), F32),
            pltpu.VMEM((512, 1536), BF),
            pltpu.VMEM((512, 1536), BF),
            pltpu.VMEM((512, 512), BF),
            pltpu.VMEM((512, 512), BF),
            pltpu.VMEM((512, 512), BF),
            pltpu.VMEM((1024, 512), BF),
            pltpu.VMEM((TOK, 512), BF),
            pltpu.VMEM((TOK, 512), BF),
            pltpu.VMEM((1024, TOK), BF),
            pltpu.VMEM((512, TOK), BF),
            pltpu.VMEM(planes, BF),
            pltpu.VMEM(planes, BF),
            pltpu.VMEM(planes, BF),
            dma((5,)),
            dma((8,)),
            dma((8,)),
            dma((CHUNKS,)),
            dma((CHUNKS,)),
            dma((CHUNKS,)),
            dma((CHUNKS,)),
            dma,
        ],
        compiler_params=pltpu.CompilerParams(
            collective_id=0, has_side_effects=True, vmem_limit_bytes=48 * 2**20
        ),
    )(
        features, conv_taps, block_gain.reshape(1, 512), grid_gain.reshape(1, 512),
        block_qkv, block_out, grid_qkv, grid_out,
    )
    return pl.pallas_call(
        unpack_kernel,
        grid=(CHUNKS,),
        out_shape=jax.ShapeDtypeStruct(features.shape, BF),
        in_specs=[pl.BlockSpec((1, PEERS, 16, 256), lambda t: (t, 0, 0, 0))],
        out_specs=pl.BlockSpec((16, 32, 512), lambda t: (0, t, 0)),
    )(returned)


def solution(mesh):
    placed = (P("rows", "cols", None), P(), P(), P(), P(), P(), P(), P())
    return jax.shard_map(
        body, mesh=mesh, in_specs=placed, out_specs=P("rows", "cols", None), check_vma=False
    )
```

```python
import jax
import jax.numpy as jnp
from jax import lax
from jax.experimental import pallas as pl
from jax.experimental.pallas import tpu as pltpu
from jax.sharding import PartitionSpec as P

MESH = pl.DeviceIdType.MESH
BF = jnp.bfloat16
F32 = jnp.float32
HEAD_DIM = 32
SCALE = HEAD_DIM ** -0.5
PEERS = 64
PIECES = 6
TOK = 256


def mm(a, b, dims=((1,), (0,))):
    return lax.dot_general(a, b, (dims, ((), ())), preferred_element_type=F32)


def norm_rows(x, gain):
    mean = jnp.mean(x, axis=-1, keepdims=True)
    cen = x - mean
    var = jnp.mean(cen * cen, axis=-1, keepdims=True)
    return (cen * lax.rsqrt(var + 1e-5) * gain).astype(BF)


def spread_heads(q):
    cols = []
    for h in range(4):
        parts = []
        if h > 0:
            parts.append(jnp.zeros((32 * h, 128), BF))
        parts.append(q[32 * h : 32 * (h + 1)])
        if h < 3:
            parts.append(jnp.zeros((32 * (3 - h), 128), BF))
        cols.append(jnp.concatenate(parts, axis=0))
    return jnp.concatenate(cols, axis=1)


def scores(unit, k_scr, qvt_scr):
    p, g = unit
    keys = k_scr[p * 128 : (p + 1) * 128, g * 128 : (g + 1) * 128]
    q = qvt_scr[g * 128 : (g + 1) * 128, p * 128 : (p + 1) * 128]
    s4 = mm(keys, spread_heads(q))
    first = lax.broadcasted_iota(jnp.int32, (64, 128), 1) < 64
    return [
        jnp.where(first, s4[:64, h * 128 : (h + 1) * 128], s4[64:, h * 128 : (h + 1) * 128])
        for h in range(4)
    ]


def soft(heads):
    lane = lax.broadcasted_iota(jnp.int32, (64, 128), 1)
    low = jnp.where(lane < 64, 1.0, 0.0).astype(BF)
    high = jnp.where(lane < 64, 0.0, 1.0).astype(BF)
    probs, inverse = [], []
    for s in heads:
        m = jnp.max(s, axis=0, keepdims=True)
        e = jnp.exp((s - m) * SCALE)
        inverse.append(1.0 / jnp.sum(e, axis=0, keepdims=True))
        pb = e.astype(BF)
        probs.append(jnp.concatenate([pb * low, pb * high], axis=0))
    return probs, inverse


def weigh(unit, softened, qvt_scr, ot_scr):
    p, g = unit
    probs, inverse = softened
    for h in range(0, 4, 2):
        r = g * 128 + h * 32
        v2 = qvt_scr[512 + r : 512 + r + 64, p * 128 : (p + 1) * 128]
        o2 = mm(v2, jnp.concatenate([probs[h], probs[h + 1]], axis=1))
        o = jnp.concatenate([o2[:32, :128] * inverse[h], o2[32:, 128:] * inverse[h + 1]], axis=0)
        ot_scr[r : r + 64, p * 128 : (p + 1) * 128] = o.astype(BF)


def attend(pairs, k_scr, qvt_scr, ot_scr):
    units = [(p, g) for p in range(pairs) for g in range(4)]
    n, b = len(units), 2
    ready = [scores(u, k_scr, qvt_scr) for u in units[:b]]
    last = None
    for i in range(0, n, b):
        now = ready
        if i + b < n:
            ready = [scores(u, k_scr, qvt_scr) for u in units[i + b : i + 2 * b]]
        done = [soft(s) for s in now]
        if last is not None:
            for u, x in zip(units[i - b : i], last):
                weigh(u, x, qvt_scr, ot_scr)
        last = done
    for u, x in zip(units[n - b :], last):
        weigh(u, x, qvt_scr, ot_scr)


def sublayer(tokens, n_scr, wk_scr, wqvt_scr, wo_scr, k_scr, qvt_scr, ot_scr):
    normed = n_scr[:tokens]
    k_scr[:tokens] = mm(normed, wk_scr[...]).astype(BF)
    qvt_scr[:, :tokens] = mm(wqvt_scr[...], normed, ((1,), (1,))).astype(BF)
    attend(tokens // 128, k_scr, qvt_scr, ot_scr)
    return mm(ot_scr[:, :tokens], wo_scr[...], ((0,), (0,)))


def to_planes(x):
    y = x.reshape(32, 8, 512)
    upper = lax.broadcasted_iota(jnp.int32, (32, 8, 128), 1) < 4
    first, second = [], []
    for lt in range(0, 4, 2):
        a, b = y[:, :, lt * 128 : (lt + 1) * 128], y[:, :, (lt + 1) * 128 : (lt + 2) * 128]
        first.append(jnp.where(upper, a, pltpu.roll(b, 4, 1)))
        second.append(jnp.where(upper, pltpu.roll(a, 4, 1), b))
    halves = [jnp.concatenate(part, axis=1) for part in (first, second)]
    return jnp.concatenate(halves, axis=0).astype(BF)


def from_planes(planes):
    p = planes.astype(F32)
    upper = lax.broadcasted_iota(jnp.int32, (32, 8, 128), 1) < 4
    tiles = []
    for k in range(0, 16, 8):
        first, second = p[:32, k : k + 8], p[32:, k : k + 8]
        tiles.append(jnp.where(upper, first, pltpu.roll(second, 4, 1)))
        tiles.append(jnp.where(upper, pltpu.roll(first, 4, 1), second))
    return jnp.concatenate(tiles, axis=2)


def main_kernel(
    feat_ref, taps_hbm, bgain_hbm, ggain_hbm, bqkv_ref, bout_ref, gqkv_ref, gout_ref,
    ret_ref,
    taps_ref, bgain_ref, ggain_ref, fpad, coll, colr, lcol, rcol, x_scr, g_scr,
    bqkv, gqkv, bwo, gwo, wk_scr, wqvt_scr, n_scr, k_scr, qvt_scr, ot_scr,
    snd, rcv, snd2,
    local_sem, halo_send, halo_recv, ssem, rsem, ssem2, rsem2, own_sem,
):
    ri, ci = lax.axis_index("rows"), lax.axis_index("cols")
    core = lax.rem(ri, 2)
    me = (ri // 2) * 8 + ci
    up, down = lax.rem(ri + 15, 16), lax.rem(ri + 1, 16)
    left, right = lax.rem(ci + 7, 8), lax.rem(ci + 1, 8)

    def device_of(unit):
        return 2 * (unit // 8) + core, lax.rem(unit, 8)

    def peer(d):
        unit = lax.rem(me + d, PEERS)
        return unit, device_of(unit)

    barrier = pltpu.get_barrier_semaphore()

    def greet(d, carry):
        pl.semaphore_signal(barrier, inc=1, device_id=peer(d)[1], device_id_type=MESH)
        return carry

    load_feat = pltpu.make_async_copy(feat_ref, fpad.at[pl.ds(1, 16)], local_sem.at[0])
    load_feat.start()
    lax.fori_loop(1, PEERS, greet, 0)
    around = [(r, c) for r in (up, down) for c in (left, ci, right)]
    for r, c in around:
        pl.semaphore_signal(barrier, inc=1, device_id=(r, c), device_id_type=MESH)
    loads = [
        pltpu.make_async_copy(src, dst, local_sem.at[i + 1])
        for i, (src, dst) in enumerate(
            (
                (taps_hbm, taps_ref), (bgain_hbm, bgain_ref), (bqkv_ref, bqkv), (bout_ref, bwo),
                (gqkv_ref, gqkv), (gout_ref, gwo), (ggain_hbm, ggain_ref),
            )
        )
    ]
    for load in loads:
        load.start()

    load_feat.wait()
    loads[0].wait()
    for r in range(16):
        coll[r : r + 1, :] = fpad[r + 1, 0:1, :]
        colr[r : r + 1, :] = fpad[r + 1, 95:96, :]
    pl.semaphore_wait(barrier, PEERS - 1 + len(around))

    halo = [
        (fpad.at[1], fpad.at[17], (up, ci)),
        (fpad.at[16], fpad.at[0], (down, ci)),
        (coll, rcol.at[1], (ri, left)),
        (colr, lcol.at[1], (ri, right)),
        (coll, rcol.at[2], (up, left)),
        (coll, rcol.at[0], (down, left)),
        (colr, lcol.at[2], (up, right)),
        (colr, lcol.at[0], (down, right)),
    ]
    halo = [
        pltpu.make_async_remote_copy(
            src, dst, halo_send.at[i], halo_recv.at[i], device_id=to, device_id_type=MESH
        )
        for i, (src, dst, to) in enumerate(halo)
    ]
    for copy in halo:
        copy.start()
    not_top, not_bottom = ri > 0, ri < 15

    def conv_row(t, r, above, below):
        half, rr = r // 8, lax.rem(r, 8)
        c0 = 32 * t
        lo, hi = max(c0 - 16, 0), min(c0 + 48, 96)
        pre, post = 8 * (t > 0), 8 * (t < 2)
        for lt in range(4):
            lanes = slice(lt * 128, (lt + 1) * 128)
            xm = fpad[r, lo:hi, lanes].astype(F32)
            x0 = fpad[r + 1, lo:hi, lanes].astype(F32)
            xp = fpad[r + 2, lo:hi, lanes].astype(F32)
            if above is not None:
                xm = jnp.where(above, xm, 0.0)
            if below is not None:
                xp = jnp.where(below, xp, 0.0)

            def column(j, start, stop):
                k = slice(start - lo, stop - lo)
                tap = [taps_ref[i : i + 1, lanes] for i in (j, j + 3, j + 6)]
                return tap[0] * xm[k] + tap[1] * x0[k] + tap[2] * xp[k]

            a0 = pltpu.roll(column(0, c0 - pre, c0 + 32), 1, 0)
            a1 = column(1, c0, c0 + 32)
            a2 = pltpu.roll(column(2, c0, c0 + 32 + post), 31 + post, 0)
            row = lax.broadcasted_iota(jnp.int32, (32, 128), 0)
            a0 = a0[8:] if pre else jnp.where(row == 0, 0.0, a0)
            a2 = a2[:32] if post else jnp.where(row == 31, 0.0, a2)
            y = x0[c0 - lo : c0 - lo + 32] + a1 + a0 + a2
            x_scr[t, half, :, rr, :, lanes] = y.reshape(4, 8, 128)

    def conv_inner(t):
        def inner(r, carry):
            conv_row(t, r, None, None)
            return carry

        lax.fori_loop(1, 15, inner, 0)

    def conv_outer(t):
        conv_row(t, 0, not_top, None)
        conv_row(t, 15, None, not_bottom)

    def conv_side(cols, arrivals, inside, k0, j, t, at):
        for i in arrivals:
            halo[i].wait_recv()
        row_of = lax.broadcasted_iota(jnp.int32, (16, 512), 0)
        sub = lax.broadcasted_iota(jnp.int32, (8, 512), 0)
        here = cols[1].astype(F32)
        before = jnp.where(not_top, cols[0].astype(F32)[15:16], 0.0)
        after = jnp.where(not_bottom, cols[2].astype(F32)[0:1], 0.0)
        shifted_m = jnp.where(row_of == 0, before, pltpu.roll(here, 1, 0))
        shifted_p = jnp.where(row_of == 15, after, pltpu.roll(here, 15, 0))
        edge = (
            taps_ref[k0 : k0 + 1, :] * shifted_m
            + taps_ref[k0 + 3 : k0 + 4, :] * here
            + taps_ref[k0 + 6 : k0 + 7, :] * shifted_p
        )
        edge = jnp.where(inside, edge, 0.0)
        for r in range(16):
            x_scr[t, r // 8, j, r % 8] += jnp.where(sub == at, edge[r : r + 1], 0.0)

    conv_inner(1)

    def prepare(wqkv, load):
        load.wait()
        wk_scr[...] = wqkv[:, 512:1024]
        wqvt_scr[:512] = wqkv[:, :512].T
        wqvt_scr[512:] = wqkv[:, 1024:].T

    prepare(bqkv, loads[2])
    conv_inner(0)
    loads[1].wait()
    loads[3].wait()

    def send_out(i, unit):
        pltpu.make_async_remote_copy(
            snd.at[i, unit], rcv.at[i, me], ssem.at[i], rsem.at[i],
            device_id=device_of(unit), device_id_type=MESH,
        ).start()

    def send_back(i, d):
        slot, device = peer(d)
        pltpu.make_async_remote_copy(
            snd2.at[i, slot], ret_ref.at[i, me], ssem2.at[i], rsem2.at[i],
            device_id=device, device_id_type=MESH,
        ).start()

    def all_of(t, src, dst, send, recv):
        return pltpu.make_async_remote_copy(
            src.at[t, pl.ds(0, PEERS - 1)], dst.at[t, pl.ds(0, PEERS - 1)], send.at[t], recv.at[t],
            device_id=(ri, ci), device_id_type=MESH,
        )

    def block(x_ref, first, count):
        tokens = TOK * count

        def rounded():
            return x_ref[...].reshape(tokens, 512).astype(BF).astype(F32)

        n_scr[:tokens] = norm_rows(rounded(), bgain_ref[...])
        out = sublayer(tokens, n_scr, wk_scr, wqvt_scr, bwo, k_scr, qvt_scr, ot_scr) + rounded()
        for j in range(count):
            i = first + j
            snd[i] = to_planes(out[j * TOK : (j + 1) * TOK])

            def start(d, c):
                send_out(i, lax.rem(me + d, PEERS))
                return c

            lax.fori_loop(1, PEERS, start, 0, unroll=9)
            rcv[i, me] = snd[i, me]

    halo[0].wait_recv()
    halo[1].wait_recv()
    conv_outer(1)

    def middle(i, carry):
        block(x_scr.at[1, i], i, 1)
        return carry

    lax.fori_loop(0, 2, middle, 0)

    def sides(i, carry):
        @pl.when(i == 0)
        def _():
            conv_outer(0)
            conv_side(lcol, (3, 6, 7), ci > 0, 0, 0, 0, 0)

        @pl.when(i == 1)
        def _():
            conv_inner(2)
            conv_outer(2)
            conv_side(rcol, (2, 4, 5), ci < 7, 2, 3, 2, 7)

        block(x_scr.at[2 * i], 2 + 2 * i, 2)
        return carry

    lax.fori_loop(0, 2, sides, 0)
    prepare(gqkv, loads[4])
    loads[5].wait()
    loads[6].wait()

    def own(i):
        return pltpu.make_async_copy(snd2.at[i, me], ret_ref.at[i, me], own_sem.at[i])

    def grid(chunk, carry):
        def place(q, lt):
            return pl.ds(1024 * (q // 4) + 4 * lt + q % 4, PEERS, stride=16)

        for j in range(2):
            i = 2 * chunk + j
            all_of(i, snd, rcv, ssem, rsem).wait_recv()
            g_scr[j * 1024 : (j + 1) * 1024] = rcv[i].astype(F32).reshape(PEERS * 16, 128)
        for q in range(8):
            window = jnp.concatenate([g_scr[place(q, lt), :] for lt in range(4)], axis=1)
            n_scr[q * 64 : (q + 1) * 64] = norm_rows(window, ggain_ref[...])
        out = sublayer(2 * TOK, n_scr, wk_scr, wqvt_scr, gwo, k_scr, qvt_scr, ot_scr)
        for q in range(8):
            for lt in range(4):
                g_scr[place(q, lt), :] += out[q * 64 : (q + 1) * 64, lt * 128 : (lt + 1) * 128]
        for j in range(2):
            i = 2 * chunk + j
            snd2[i] = g_scr[j * 1024 : (j + 1) * 1024].reshape(PEERS, 16, 128).astype(BF)

            def start(d, c):
                send_back(i, d)
                return c

            lax.fori_loop(1, PEERS, start, 0, unroll=9)
            own(i).start()
        return carry

    lax.fori_loop(0, PIECES // 2, grid, 0)

    for copy in halo:
        copy.wait_send()
    for t in range(PIECES):
        all_of(t, snd, rcv, ssem, rsem).wait_send()
    for t in range(PIECES):
        back = all_of(t, snd2, ret_ref, ssem2, rsem2)
        back.wait_send()
        back.wait_recv()
        own(t).wait()


def unpack_kernel(ret_ref, out_ref, planes, frame, in_sem, out_sem):
    pieces = [(t, half) for t in (1, 0, 2) for half in range(2)]
    arrive = [
        pltpu.make_async_copy(ret_ref.at[i], planes.at[i], in_sem.at[i]) for i in range(PIECES)
    ]
    for copy in arrive:
        copy.start()
    leave = []
    for i, (t, half) in enumerate(pieces):
        arrive[i].wait()
        y = from_planes(planes[i]).reshape(4, 8, 8, 512).transpose(1, 0, 2, 3)
        frame[i] = y.reshape(8, 32, 512).astype(BF)
        place = out_ref.at[pl.ds(8 * half, 8), pl.ds(32 * t, 32)]
        leave.append(pltpu.make_async_copy(frame.at[i], place, out_sem.at[i]))
        leave[-1].start()
    for copy in leave:
        copy.wait()


def body(features, conv_taps, block_gain, block_qkv, block_out, grid_gain, grid_qkv, grid_out):
    any_ = pl.BlockSpec(memory_space=pl.ANY)
    dma = pltpu.SemaphoreType.DMA
    planes = (PIECES, PEERS, 16, 128)
    returned = pl.pallas_call(
        main_kernel,
        out_shape=jax.ShapeDtypeStruct(planes, BF),
        in_specs=[any_] * 8,
        out_specs=any_,
        scratch_shapes=[
            pltpu.VMEM((9, 512), F32),
            pltpu.VMEM((1, 512), F32),
            pltpu.VMEM((1, 512), F32),
            pltpu.VMEM((18, 96, 512), BF),
            pltpu.VMEM((16, 512), BF),
            pltpu.VMEM((16, 512), BF),
            pltpu.VMEM((3, 16, 512), BF),
            pltpu.VMEM((3, 16, 512), BF),
            pltpu.VMEM((3, 2, 4, 8, 8, 512), F32),
            pltpu.VMEM((2 * PEERS * 16, 128), F32),
            pltpu.VMEM((512, 1536), BF),
            pltpu.VMEM((512, 1536), BF),
            pltpu.VMEM((512, 512), BF),
            pltpu.VMEM((512, 512), BF),
            pltpu.VMEM((512, 512), BF),
            pltpu.VMEM((1024, 512), BF),
            pltpu.VMEM((2 * TOK, 512), BF),
            pltpu.VMEM((2 * TOK, 512), BF),
            pltpu.VMEM((1024, 2 * TOK), BF),
            pltpu.VMEM((512, 2 * TOK), BF),
            pltpu.VMEM(planes, BF),
            pltpu.VMEM(planes, BF),
            pltpu.VMEM(planes, BF),
            dma((8,)),
            dma((8,)),
            dma((8,)),
            dma((PIECES,)),
            dma((PIECES,)),
            dma((PIECES,)),
            dma((PIECES,)),
            dma((PIECES,)),
        ],
        compiler_params=pltpu.CompilerParams(
            collective_id=0, has_side_effects=True, vmem_limit_bytes=60 * 2**20
        ),
    )(
        features, conv_taps, block_gain.reshape(1, 512), grid_gain.reshape(1, 512),
        block_qkv, block_out, grid_qkv, grid_out,
    )
    return pl.pallas_call(
        unpack_kernel,
        out_shape=jax.ShapeDtypeStruct(features.shape, BF),
        in_specs=[any_],
        out_specs=any_,
        scratch_shapes=[
            pltpu.VMEM(planes, BF),
            pltpu.VMEM((PIECES, 8, 32, 512), BF),
            dma((PIECES,)),
            dma((PIECES,)),
        ],
        compiler_params=pltpu.CompilerParams(vmem_limit_bytes=60 * 2**20),
    )(returned)


def solution(mesh):
    placed = (P("rows", "cols", None), P(), P(), P(), P(), P(), P(), P())
    return jax.shard_map(
        body, mesh=mesh, in_specs=placed, out_specs=P("rows", "cols", None), check_vma=False
    )
```

```python
import jax
import jax.numpy as jnp
from jax import lax
from jax.experimental import pallas as pl
from jax.experimental.pallas import tpu as pltpu
from jax.sharding import PartitionSpec as P

MESH = pl.DeviceIdType.MESH
BF = jnp.bfloat16
F32 = jnp.float32
HEAD_DIM = 32
SCALE = HEAD_DIM ** -0.5
PEERS = 64
CHUNKS = 3
TOK = 256


def mm(a, b, dims=((1,), (0,))):
    return lax.dot_general(a, b, (dims, ((), ())), preferred_element_type=F32)


def norm_rows(x, gain):
    mean = jnp.mean(x, axis=-1, keepdims=True)
    cen = x - mean
    var = jnp.mean(cen * cen, axis=-1, keepdims=True)
    return (cen * lax.rsqrt(var + 1e-5) * gain).astype(BF)


def spread_heads(q):
    cols = []
    for h in range(4):
        parts = []
        if h > 0:
            parts.append(jnp.zeros((32 * h, 128), BF))
        parts.append(q[32 * h : 32 * (h + 1)])
        if h < 3:
            parts.append(jnp.zeros((32 * (3 - h), 128), BF))
        cols.append(jnp.concatenate(parts, axis=0))
    return jnp.concatenate(cols, axis=1)


def scores(unit, k_scr, qvt_scr):
    p, g = unit
    keys = k_scr[p * 128 : (p + 1) * 128, g * 128 : (g + 1) * 128]
    q = qvt_scr[g * 128 : (g + 1) * 128, p * 128 : (p + 1) * 128]
    s4 = mm(keys, spread_heads(q))
    first = lax.broadcasted_iota(jnp.int32, (64, 128), 1) < 64
    return [
        jnp.where(first, s4[:64, h * 128 : (h + 1) * 128], s4[64:, h * 128 : (h + 1) * 128])
        for h in range(4)
    ]


def soft(heads):
    lane = lax.broadcasted_iota(jnp.int32, (64, 128), 1)
    low = jnp.where(lane < 64, 1.0, 0.0).astype(BF)
    high = jnp.where(lane < 64, 0.0, 1.0).astype(BF)
    probs, inverse = [], []
    for s in heads:
        m = jnp.max(s, axis=0, keepdims=True)
        e = jnp.exp((s - m) * SCALE)
        inverse.append(1.0 / jnp.sum(e, axis=0, keepdims=True))
        pb = e.astype(BF)
        probs.append(jnp.concatenate([pb * low, pb * high], axis=0))
    return probs, inverse


def weigh(unit, softened, qvt_scr, ot_scr):
    p, g = unit
    probs, inverse = softened
    for h in range(0, 4, 2):
        r = g * 128 + h * 32
        v2 = qvt_scr[512 + r : 512 + r + 64, p * 128 : (p + 1) * 128]
        o2 = mm(v2, jnp.concatenate([probs[h], probs[h + 1]], axis=1))
        o = jnp.concatenate([o2[:32, :128] * inverse[h], o2[32:, 128:] * inverse[h + 1]], axis=0)
        ot_scr[r : r + 64, p * 128 : (p + 1) * 128] = o.astype(BF)


def attend(pairs, k_scr, qvt_scr, ot_scr):
    units = [(p, g) for p in range(pairs) for g in range(4)]
    n, b = len(units), 2
    ready = [scores(u, k_scr, qvt_scr) for u in units[:b]]
    last = None
    for i in range(0, n, b):
        now = ready
        if i + b < n:
            ready = [scores(u, k_scr, qvt_scr) for u in units[i + b : i + 2 * b]]
        done = [soft(s) for s in now]
        if last is not None:
            for u, x in zip(units[i - b : i], last):
                weigh(u, x, qvt_scr, ot_scr)
        last = done
    for u, x in zip(units[n - b :], last):
        weigh(u, x, qvt_scr, ot_scr)


def sublayer(tokens, n_scr, wk_scr, wqvt_scr, wo_scr, k_scr, qvt_scr, ot_scr):
    normed = n_scr[:tokens]
    k_scr[:tokens] = mm(normed, wk_scr[...]).astype(BF)
    qvt_scr[:, :tokens] = mm(wqvt_scr[...], normed, ((1,), (1,))).astype(BF)
    attend(tokens // 128, k_scr, qvt_scr, ot_scr)
    return mm(ot_scr[:, :tokens], wo_scr[...], ((0,), (0,)))


def to_planes(x):
    y = x.reshape(32, 8, 512)
    upper = lax.broadcasted_iota(jnp.int32, (32, 8, 128), 1) < 4
    first, second = [], []
    for lt in range(0, 4, 2):
        a, b = y[:, :, lt * 128 : (lt + 1) * 128], y[:, :, (lt + 1) * 128 : (lt + 2) * 128]
        first.append(jnp.where(upper, a, pltpu.roll(b, 4, 1)))
        second.append(jnp.where(upper, pltpu.roll(a, 4, 1), b))
    halves = [jnp.concatenate(part, axis=1) for part in (first, second)]
    return jnp.concatenate(halves, axis=0).astype(BF)


def from_planes(planes):
    p = planes.astype(F32)
    upper = lax.broadcasted_iota(jnp.int32, (32, 8, 128), 1) < 4
    tiles = []
    for k in range(0, 16, 8):
        first, second = p[:32, k : k + 8], p[32:, k : k + 8]
        tiles.append(jnp.where(upper, first, pltpu.roll(second, 4, 1)))
        tiles.append(jnp.where(upper, pltpu.roll(first, 4, 1), second))
    return jnp.concatenate(tiles, axis=2)


def main_kernel(
    feat_ref, taps_hbm, bgain_hbm, ggain_hbm, bqkv_ref, bout_ref, gqkv_ref, gout_ref,
    ret_ref,
    taps_ref, bgain_ref, ggain_ref, fpad, coll, colr, lcol, rcol, x_scr, g_scr,
    bqkv, gqkv, bwo, gwo, wk_scr, wqvt_scr, n_scr, k_scr, qvt_scr, ot_scr,
    snd, rcv, snd2,
    local_sem, halo_send, halo_recv, ssem, rsem, ssem2, rsem2, own_sem,
):
    ri, ci = lax.axis_index("rows"), lax.axis_index("cols")
    core = lax.rem(ri, 2)
    me = (ri // 2) * 8 + ci
    up, down = lax.rem(ri + 15, 16), lax.rem(ri + 1, 16)
    left, right = lax.rem(ci + 7, 8), lax.rem(ci + 1, 8)

    def device_of(unit):
        return 2 * (unit // 8) + core, lax.rem(unit, 8)

    def peer(d):
        unit = lax.rem(me + d, PEERS)
        return unit, device_of(unit)

    barrier = pltpu.get_barrier_semaphore()

    def greet(d, carry):
        pl.semaphore_signal(barrier, inc=1, device_id=peer(d)[1], device_id_type=MESH)
        return carry

    load_feat = pltpu.make_async_copy(feat_ref, fpad.at[pl.ds(1, 16)], local_sem.at[0])
    load_feat.start()
    lax.fori_loop(1, PEERS, greet, 0)
    around = [(r, c) for r in (up, down) for c in (left, ci, right)]
    for r, c in around:
        pl.semaphore_signal(barrier, inc=1, device_id=(r, c), device_id_type=MESH)
    loads = [
        pltpu.make_async_copy(src, dst, local_sem.at[i + 1])
        for i, (src, dst) in enumerate(
            (
                (taps_hbm, taps_ref), (bgain_hbm, bgain_ref), (bqkv_ref, bqkv), (bout_ref, bwo),
                (gqkv_ref, gqkv), (gout_ref, gwo), (ggain_hbm, ggain_ref),
            )
        )
    ]
    for load in loads:
        load.start()

    load_feat.wait()
    loads[0].wait()
    for r in range(16):
        coll[r : r + 1, :] = fpad[r + 1, 0:1, :]
        colr[r : r + 1, :] = fpad[r + 1, 95:96, :]
    pl.semaphore_wait(barrier, PEERS - 1 + len(around))

    halo = [
        (fpad.at[1, pl.ds(16, 64)], fpad.at[17, pl.ds(16, 64)], (up, ci)),
        (fpad.at[16, pl.ds(16, 64)], fpad.at[0, pl.ds(16, 64)], (down, ci)),
        (coll, rcol.at[1], (ri, left)),
        (colr, lcol.at[1], (ri, right)),
        (coll, rcol.at[2], (up, left)),
        (coll, rcol.at[0], (down, left)),
        (colr, lcol.at[2], (up, right)),
        (colr, lcol.at[0], (down, right)),
        (fpad.at[1, pl.ds(0, 16)], fpad.at[17, pl.ds(0, 16)], (up, ci)),
        (fpad.at[16, pl.ds(0, 16)], fpad.at[0, pl.ds(0, 16)], (down, ci)),
        (fpad.at[1, pl.ds(80, 16)], fpad.at[17, pl.ds(80, 16)], (up, ci)),
        (fpad.at[16, pl.ds(80, 16)], fpad.at[0, pl.ds(80, 16)], (down, ci)),
    ]
    halo = [
        pltpu.make_async_remote_copy(
            src, dst, halo_send.at[i], halo_recv.at[i], device_id=to, device_id_type=MESH
        )
        for i, (src, dst, to) in enumerate(halo)
    ]
    for copy in halo:
        copy.start()
    not_top, not_bottom = ri > 0, ri < 15

    def conv_row(t, r, above, below):
        half, rr = r // 8, lax.rem(r, 8)
        c0 = 32 * t
        lo, hi = max(c0 - 16, 0), min(c0 + 48, 96)
        pre, post = 8 * (t > 0), 8 * (t < 2)
        for lt in range(4):
            lanes = slice(lt * 128, (lt + 1) * 128)
            xm = fpad[r, lo:hi, lanes].astype(F32)
            x0 = fpad[r + 1, lo:hi, lanes].astype(F32)
            xp = fpad[r + 2, lo:hi, lanes].astype(F32)
            if above is not None:
                xm = jnp.where(above, xm, 0.0)
            if below is not None:
                xp = jnp.where(below, xp, 0.0)

            def column(j, start, stop):
                k = slice(start - lo, stop - lo)
                tap = [taps_ref[i : i + 1, lanes] for i in (j, j + 3, j + 6)]
                return tap[0] * xm[k] + tap[1] * x0[k] + tap[2] * xp[k]

            a0 = pltpu.roll(column(0, c0 - pre, c0 + 32), 1, 0)
            a1 = column(1, c0, c0 + 32)
            a2 = pltpu.roll(column(2, c0, c0 + 32 + post), 31 + post, 0)
            row = lax.broadcasted_iota(jnp.int32, (32, 128), 0)
            a0 = a0[8:] if pre else jnp.where(row == 0, 0.0, a0)
            a2 = a2[:32] if post else jnp.where(row == 31, 0.0, a2)
            y = x0[c0 - lo : c0 - lo + 32] + a1 + a0 + a2
            x_scr[t, half, :, rr, :, lanes] = y.reshape(4, 8, 128)

    def conv_inner(t):
        def inner(r, carry):
            conv_row(t, r, None, None)
            return carry

        lax.fori_loop(1, 15, inner, 0)

    def conv_outer(t):
        conv_row(t, 0, not_top, None)
        conv_row(t, 15, None, not_bottom)

    def conv_side(cols, arrivals, inside, k0, j, t, at):
        for i in arrivals:
            halo[i].wait_recv()
        row_of = lax.broadcasted_iota(jnp.int32, (16, 512), 0)
        sub = lax.broadcasted_iota(jnp.int32, (8, 512), 0)
        here = cols[1].astype(F32)
        before = jnp.where(not_top, cols[0].astype(F32)[15:16], 0.0)
        after = jnp.where(not_bottom, cols[2].astype(F32)[0:1], 0.0)
        shifted_m = jnp.where(row_of == 0, before, pltpu.roll(here, 1, 0))
        shifted_p = jnp.where(row_of == 15, after, pltpu.roll(here, 15, 0))
        edge = (
            taps_ref[k0 : k0 + 1, :] * shifted_m
            + taps_ref[k0 + 3 : k0 + 4, :] * here
            + taps_ref[k0 + 6 : k0 + 7, :] * shifted_p
        )
        edge = jnp.where(inside, edge, 0.0)
        for r in range(16):
            x_scr[t, r // 8, j, r % 8] += jnp.where(sub == at, edge[r : r + 1], 0.0)

    conv_inner(1)

    def prepare(wqkv, load):
        load.wait()
        wk_scr[...] = wqkv[:, 512:1024]
        wqvt_scr[:512] = wqkv[:, :512].T
        wqvt_scr[512:] = wqkv[:, 1024:].T

    prepare(bqkv, loads[2])
    conv_inner(0)
    loads[1].wait()
    loads[3].wait()

    def send_out(i, unit, rows):
        pltpu.make_async_remote_copy(
            snd.at[i, unit, rows], rcv.at[i, me, rows], ssem.at[i], rsem.at[i],
            device_id=device_of(unit), device_id_type=MESH,
        ).start()

    def send_back(i, d):
        slot, device = peer(d)
        pltpu.make_async_remote_copy(
            snd2.at[i, slot], ret_ref.at[i, me], ssem2.at[i], rsem2.at[i],
            device_id=device, device_id_type=MESH,
        ).start()

    def all_of(t, src, dst, send, recv):
        return pltpu.make_async_remote_copy(
            src.at[t, pl.ds(0, PEERS - 1)], dst.at[t, pl.ds(0, PEERS - 1)], send.at[t], recv.at[t],
            device_id=(ri, ci), device_id_type=MESH,
        )

    def block(x_ref, i, count, row):
        tokens = TOK * count

        def rounded():
            return x_ref[...].reshape(tokens, 512).astype(BF).astype(F32)

        n_scr[:tokens] = norm_rows(rounded(), bgain_ref[...])
        out = sublayer(tokens, n_scr, wk_scr, wqvt_scr, bwo, k_scr, qvt_scr, ot_scr) + rounded()
        for j in range(count):
            snd[i, :, pl.ds(row + 16 * j, 16), :] = to_planes(out[j * TOK : (j + 1) * TOK])
        rows = pl.ds(row, 16 * count)

        def start(d, c):
            send_out(i, lax.rem(me + d, PEERS), rows)
            return c

        lax.fori_loop(1, PEERS, start, 0, unroll=9)
        rcv[i, me, rows, :] = snd[i, me, rows, :]

    conv_inner(2)
    halo[0].wait_recv()
    halo[1].wait_recv()
    conv_outer(1)

    def middle(i, carry):
        block(x_scr.at[1, i], 0, 1, pl.multiple_of(16 * i, 16))
        return carry

    lax.fori_loop(0, 2, middle, 0)

    def sides(i, carry):
        @pl.when(i == 0)
        def _():
            halo[8].wait_recv()
            halo[9].wait_recv()
            conv_outer(0)
            conv_side(lcol, (3, 6, 7), ci > 0, 0, 0, 0, 0)

        @pl.when(i == 1)
        def _():
            halo[10].wait_recv()
            halo[11].wait_recv()
            conv_outer(2)
            conv_side(rcol, (2, 4, 5), ci < 7, 2, 3, 2, 7)

        block(x_scr.at[2 * i], 1 + i, 2, 0)
        return carry

    lax.fori_loop(0, 2, sides, 0)
    prepare(gqkv, loads[4])
    loads[5].wait()
    loads[6].wait()

    def own(i):
        return pltpu.make_async_copy(snd2.at[i, me], ret_ref.at[i, me], own_sem.at[i])

    def grid(i, carry):
        def place(q, lt):
            return pl.ds(16 * (q // 4) + 4 * lt + q % 4, PEERS, stride=32)

        all_of(i, snd, rcv, ssem, rsem).wait_recv()
        g_scr[...] = rcv[i].astype(F32).reshape(PEERS * 32, 128)
        for q in range(8):
            window = jnp.concatenate([g_scr[place(q, lt), :] for lt in range(4)], axis=1)
            n_scr[q * 64 : (q + 1) * 64] = norm_rows(window, ggain_ref[...])
        out = sublayer(2 * TOK, n_scr, wk_scr, wqvt_scr, gwo, k_scr, qvt_scr, ot_scr)
        for q in range(8):
            for lt in range(4):
                g_scr[place(q, lt), :] += out[q * 64 : (q + 1) * 64, lt * 128 : (lt + 1) * 128]
        snd2[i] = g_scr[...].reshape(PEERS, 32, 128).astype(BF)

        def start(d, c):
            send_back(i, d)
            return c

        lax.fori_loop(1, PEERS, start, 0, unroll=9)
        own(i).start()
        return carry

    lax.fori_loop(0, CHUNKS, grid, 0)

    for copy in halo:
        copy.wait_send()
    for t in range(CHUNKS):
        all_of(t, snd, rcv, ssem, rsem).wait_send()
    for t in range(CHUNKS):
        back = all_of(t, snd2, ret_ref, ssem2, rsem2)
        back.wait_send()
        back.wait_recv()
        own(t).wait()


def unpack_kernel(ret_ref, out_ref, frame, out_sem):
    leave = []
    for i, (t, half) in enumerate([(t, half) for t in (1, 0, 2) for half in range(2)]):
        y = from_planes(ret_ref[i // 2, :, 16 * half : 16 * half + 16, :]).reshape(4, 8, 8, 512)
        frame[i] = y.transpose(1, 0, 2, 3).reshape(8, 32, 512).astype(BF)
        place = out_ref.at[pl.ds(8 * half, 8), pl.ds(32 * t, 32)]
        leave.append(pltpu.make_async_copy(frame.at[i], place, out_sem.at[i]))
        leave[-1].start()
    for copy in leave:
        copy.wait()


def body(features, conv_taps, block_gain, block_qkv, block_out, grid_gain, grid_qkv, grid_out):
    any_ = pl.BlockSpec(memory_space=pl.ANY)
    vmem = pl.BlockSpec(memory_space=pltpu.VMEM)
    dma = pltpu.SemaphoreType.DMA
    planes = (CHUNKS, PEERS, 32, 128)
    returned = pl.pallas_call(
        main_kernel,
        out_shape=pltpu.VMEM(planes, BF),
        in_specs=[any_] * 8,
        out_specs=vmem,
        scratch_shapes=[
            pltpu.VMEM((9, 512), F32),
            pltpu.VMEM((1, 512), F32),
            pltpu.VMEM((1, 512), F32),
            pltpu.VMEM((18, 96, 512), BF),
            pltpu.VMEM((16, 512), BF),
            pltpu.VMEM((16, 512), BF),
            pltpu.VMEM((3, 16, 512), BF),
            pltpu.VMEM((3, 16, 512), BF),
            pltpu.VMEM((3, 2, 4, 8, 8, 512), F32),
            pltpu.VMEM((2 * PEERS * 16, 128), F32),
            pltpu.VMEM((512, 1536), BF),
            pltpu.VMEM((512, 1536), BF),
            pltpu.VMEM((512, 512), BF),
            pltpu.VMEM((512, 512), BF),
            pltpu.VMEM((512, 512), BF),
            pltpu.VMEM((1024, 512), BF),
            pltpu.VMEM((2 * TOK, 512), BF),
            pltpu.VMEM((2 * TOK, 512), BF),
            pltpu.VMEM((1024, 2 * TOK), BF),
            pltpu.VMEM((512, 2 * TOK), BF),
            pltpu.VMEM(planes, BF),
            pltpu.VMEM(planes, BF),
            pltpu.VMEM(planes, BF),
            dma((8,)),
            dma((12,)),
            dma((12,)),
            dma((CHUNKS,)),
            dma((CHUNKS,)),
            dma((CHUNKS,)),
            dma((CHUNKS,)),
            dma((CHUNKS,)),
        ],
        compiler_params=pltpu.CompilerParams(
            collective_id=0, has_side_effects=True, vmem_limit_bytes=60 * 2**20
        ),
    )(
        features, conv_taps, block_gain.reshape(1, 512), grid_gain.reshape(1, 512),
        block_qkv, block_out, grid_qkv, grid_out,
    )
    return pl.pallas_call(
        unpack_kernel,
        out_shape=jax.ShapeDtypeStruct(features.shape, BF),
        in_specs=[vmem],
        out_specs=any_,
        scratch_shapes=[
            pltpu.VMEM((2 * CHUNKS, 8, 32, 512), BF),
            dma((2 * CHUNKS,)),
        ],
        compiler_params=pltpu.CompilerParams(vmem_limit_bytes=16 * 2**20),
    )(returned)


def solution(mesh):
    placed = (P("rows", "cols", None), P(), P(), P(), P(), P(), P(), P())
    return jax.shard_map(
        body, mesh=mesh, in_specs=placed, out_specs=P("rows", "cols", None), check_vma=False
    )
```

```python
import jax
import jax.numpy as jnp
from jax import lax
from jax.experimental import pallas as pl
from jax.experimental.pallas import tpu as pltpu
from jax.sharding import PartitionSpec as P

MESH = pl.DeviceIdType.MESH
BF = jnp.bfloat16
F32 = jnp.float32
HEAD_DIM = 32
SCALE = HEAD_DIM ** -0.5
PEERS = 64
CHUNKS = 3
TOK = 256


def mm(a, b, dims=((1,), (0,))):
    return lax.dot_general(a, b, (dims, ((), ())), preferred_element_type=F32)


def norm_rows(x, gain):
    mean = jnp.mean(x, axis=-1, keepdims=True)
    cen = x - mean
    var = jnp.mean(cen * cen, axis=-1, keepdims=True)
    return (cen * lax.rsqrt(var + 1e-5) * gain).astype(BF)


def spread_heads(q):
    cols = []
    for h in range(4):
        parts = []
        if h > 0:
            parts.append(jnp.zeros((32 * h, 128), BF))
        parts.append(q[32 * h : 32 * (h + 1)])
        if h < 3:
            parts.append(jnp.zeros((32 * (3 - h), 128), BF))
        cols.append(jnp.concatenate(parts, axis=0))
    return jnp.concatenate(cols, axis=1)


def scores(unit, k_scr, qvt_scr):
    p, g = unit
    keys = k_scr[p * 128 : (p + 1) * 128, g * 128 : (g + 1) * 128]
    q = qvt_scr[g * 128 : (g + 1) * 128, p * 128 : (p + 1) * 128]
    s4 = mm(keys, spread_heads(q))
    first = lax.broadcasted_iota(jnp.int32, (64, 128), 1) < 64
    return [
        jnp.where(first, s4[:64, h * 128 : (h + 1) * 128], s4[64:, h * 128 : (h + 1) * 128])
        for h in range(4)
    ]


def soft(heads):
    lane = lax.broadcasted_iota(jnp.int32, (64, 128), 1)
    low = jnp.where(lane < 64, 1.0, 0.0).astype(BF)
    high = jnp.where(lane < 64, 0.0, 1.0).astype(BF)
    probs, inverse = [], []
    for s in heads:
        m = jnp.max(s, axis=0, keepdims=True)
        e = jnp.exp((s - m) * SCALE)
        inverse.append(1.0 / jnp.sum(e, axis=0, keepdims=True))
        pb = e.astype(BF)
        probs.append(jnp.concatenate([pb * low, pb * high], axis=0))
    return probs, inverse


def weigh(unit, softened, qvt_scr, ot_scr):
    p, g = unit
    probs, inverse = softened
    for h in range(0, 4, 2):
        r = g * 128 + h * 32
        v2 = qvt_scr[512 + r : 512 + r + 64, p * 128 : (p + 1) * 128]
        o2 = mm(v2, jnp.concatenate([probs[h], probs[h + 1]], axis=1))
        o = jnp.concatenate([o2[:32, :128] * inverse[h], o2[32:, 128:] * inverse[h + 1]], axis=0)
        ot_scr[r : r + 64, p * 128 : (p + 1) * 128] = o.astype(BF)


def sublayer(tokens, n_scr, wk_scr, wqvt_scr, wo_scr, k_scr, qvt_scr, ot_scr):
    tok = slice(0, tokens)
    normed = n_scr[tok]

    def project(first, size):
        rows = slice(first, first + size)
        qvt_scr[rows, tok] = mm(wqvt_scr[rows], normed, ((1,), (1,))).astype(BF)

    def keys(first):
        cols = slice(first, first + 256)
        k_scr[tok, cols] = mm(normed, wk_scr[:, cols]).astype(BF)

    pairs, b = tokens // 128, 2
    units = [(p, g) for half in range(2) for p in range(pairs) for g in (2 * half, 2 * half + 1)]
    n = len(units)
    keys(0)
    project(0, 256)
    ready = [scores(u, k_scr, qvt_scr) for u in units[:b]]
    project(512, 256)
    last, later = None, [lambda: keys(256), lambda: project(256, 256), lambda: project(768, 256)]
    out = None
    for i in range(0, n, b):
        now = ready
        if i // b >= n // (2 * b) - len(later) - 1:
            while later and i // b >= n // (2 * b) - len(later) - 1:
                later.pop(0)()
        if i + b < n:
            ready = [scores(u, k_scr, qvt_scr) for u in units[i + b : i + 2 * b]]
        done = [soft(s) for s in now]
        if last is not None:
            for u, x in zip(units[i - b : i], last):
                weigh(u, x, qvt_scr, ot_scr)
        last = done
        if i == n // 2 + b:
            out = mm(ot_scr[:256, tok], wo_scr[:256], ((0,), (0,)))
    for u, x in zip(units[n - b :], last):
        weigh(u, x, qvt_scr, ot_scr)
    return out + mm(ot_scr[256:, tok], wo_scr[256:], ((0,), (0,)))


def to_planes(x):
    y = x.reshape(32, 8, 512)
    upper = lax.broadcasted_iota(jnp.int32, (32, 8, 128), 1) < 4
    first, second = [], []
    for lt in range(0, 4, 2):
        a, b = y[:, :, lt * 128 : (lt + 1) * 128], y[:, :, (lt + 1) * 128 : (lt + 2) * 128]
        first.append(jnp.where(upper, a, pltpu.roll(b, 4, 1)))
        second.append(jnp.where(upper, pltpu.roll(a, 4, 1), b))
    halves = [jnp.concatenate(part, axis=1) for part in (first, second)]
    return jnp.concatenate(halves, axis=0).astype(BF)


def from_planes(planes):
    p = planes.astype(F32)
    upper = lax.broadcasted_iota(jnp.int32, (32, 8, 128), 1) < 4
    tiles = []
    for k in range(0, 16, 8):
        first, second = p[:32, k : k + 8], p[32:, k : k + 8]
        tiles.append(jnp.where(upper, first, pltpu.roll(second, 4, 1)))
        tiles.append(jnp.where(upper, pltpu.roll(first, 4, 1), second))
    return jnp.concatenate(tiles, axis=2)


def main_kernel(
    feat_ref, taps_hbm, bgain_hbm, ggain_hbm, bqkv_ref, bout_ref, gqkv_ref, gout_ref,
    ret_ref,
    taps_ref, bgain_ref, ggain_ref, fpad, coll, colr, lcol, rcol, x_scr, g_scr,
    bqkv, gqkv, bwo, gwo, wk_scr, wqvt_scr, n_scr, n_mid, k_scr, qvt_scr, ot_scr,
    snd, rcv, snd2,
    local_sem, halo_send, halo_recv, ssem, rsem, ssem2, rsem2, own_sem,
):
    ri, ci = lax.axis_index("rows"), lax.axis_index("cols")
    core = lax.rem(ri, 2)
    me = (ri // 2) * 8 + ci
    up, down = lax.rem(ri + 15, 16), lax.rem(ri + 1, 16)
    left, right = lax.rem(ci + 7, 8), lax.rem(ci + 1, 8)

    def device_of(unit):
        return 2 * (unit // 8) + core, lax.rem(unit, 8)

    def peer(d):
        unit = lax.rem(me + d, PEERS)
        return unit, device_of(unit)

    barrier = pltpu.get_barrier_semaphore()

    def greet(d, carry):
        pl.semaphore_signal(barrier, inc=1, device_id=peer(d)[1], device_id_type=MESH)
        return carry

    load_feat = pltpu.make_async_copy(feat_ref, fpad.at[pl.ds(1, 16)], local_sem.at[0])
    load_feat.start()
    lax.fori_loop(1, PEERS, greet, 0)
    around = [(r, c) for r in (up, down) for c in (left, ci, right)]
    for r, c in around:
        pl.semaphore_signal(barrier, inc=1, device_id=(r, c), device_id_type=MESH)
    loads = [
        pltpu.make_async_copy(src, dst, local_sem.at[i + 1])
        for i, (src, dst) in enumerate(
            (
                (taps_hbm, taps_ref), (bgain_hbm, bgain_ref), (bqkv_ref, bqkv), (bout_ref, bwo),
                (gqkv_ref, gqkv), (gout_ref, gwo), (ggain_hbm, ggain_ref),
            )
        )
    ]
    for load in loads:
        load.start()

    load_feat.wait()
    loads[0].wait()
    for r in range(16):
        coll[r : r + 1, :] = fpad[r + 1, 0:1, :]
        colr[r : r + 1, :] = fpad[r + 1, 95:96, :]
    pl.semaphore_wait(barrier, PEERS - 1 + len(around))

    halo = [
        (fpad.at[1, pl.ds(16, 64)], fpad.at[17, pl.ds(16, 64)], (up, ci)),
        (fpad.at[16, pl.ds(16, 64)], fpad.at[0, pl.ds(16, 64)], (down, ci)),
        (coll, rcol.at[1], (ri, left)),
        (colr, lcol.at[1], (ri, right)),
        (coll, rcol.at[2], (up, left)),
        (coll, rcol.at[0], (down, left)),
        (colr, lcol.at[2], (up, right)),
        (colr, lcol.at[0], (down, right)),
        (fpad.at[1, pl.ds(0, 16)], fpad.at[17, pl.ds(0, 16)], (up, ci)),
        (fpad.at[16, pl.ds(0, 16)], fpad.at[0, pl.ds(0, 16)], (down, ci)),
        (fpad.at[1, pl.ds(80, 16)], fpad.at[17, pl.ds(80, 16)], (up, ci)),
        (fpad.at[16, pl.ds(80, 16)], fpad.at[0, pl.ds(80, 16)], (down, ci)),
    ]
    halo = [
        pltpu.make_async_remote_copy(
            src, dst, halo_send.at[i], halo_recv.at[i], device_id=to, device_id_type=MESH
        )
        for i, (src, dst, to) in enumerate(halo)
    ]
    for copy in halo:
        copy.start()
    not_top, not_bottom = ri > 0, ri < 15

    def conv_row(t, r, above, below):
        half, rr = r // 8, lax.rem(r, 8)
        c0 = 32 * t
        lo, hi = max(c0 - 16, 0), min(c0 + 48, 96)
        pre, post = 8 * (t > 0), 8 * (t < 2)
        for lt in range(4):
            lanes = slice(lt * 128, (lt + 1) * 128)
            xm = fpad[r, lo:hi, lanes].astype(F32)
            x0 = fpad[r + 1, lo:hi, lanes].astype(F32)
            xp = fpad[r + 2, lo:hi, lanes].astype(F32)
            if above is not None:
                xm = jnp.where(above, xm, 0.0)
            if below is not None:
                xp = jnp.where(below, xp, 0.0)

            def column(j, start, stop):
                k = slice(start - lo, stop - lo)
                tap = [taps_ref[i : i + 1, lanes] for i in (j, j + 3, j + 6)]
                return tap[0] * xm[k] + tap[1] * x0[k] + tap[2] * xp[k]

            a0 = pltpu.roll(column(0, c0 - pre, c0 + 32), 1, 0)
            a1 = column(1, c0, c0 + 32)
            a2 = pltpu.roll(column(2, c0, c0 + 32 + post), 31 + post, 0)
            row = lax.broadcasted_iota(jnp.int32, (32, 128), 0)
            a0 = a0[8:] if pre else jnp.where(row == 0, 0.0, a0)
            a2 = a2[:32] if post else jnp.where(row == 31, 0.0, a2)
            y = x0[c0 - lo : c0 - lo + 32] + a1 + a0 + a2
            x_scr[t, half, :, rr, :, lanes] = y.reshape(4, 8, 128)

    def conv_inner(t):
        def inner(r, carry):
            conv_row(t, r, None, None)
            return carry

        lax.fori_loop(1, 15, inner, 0)

    def conv_outer(t):
        conv_row(t, 0, not_top, None)
        conv_row(t, 15, None, not_bottom)

    def conv_side(cols, arrivals, inside, k0, j, t, at):
        for i in arrivals:
            halo[i].wait_recv()
        row_of = lax.broadcasted_iota(jnp.int32, (16, 512), 0)
        sub = lax.broadcasted_iota(jnp.int32, (8, 512), 0)
        here = cols[1].astype(F32)
        before = jnp.where(not_top, cols[0].astype(F32)[15:16], 0.0)
        after = jnp.where(not_bottom, cols[2].astype(F32)[0:1], 0.0)
        shifted_m = jnp.where(row_of == 0, before, pltpu.roll(here, 1, 0))
        shifted_p = jnp.where(row_of == 15, after, pltpu.roll(here, 15, 0))
        edge = (
            taps_ref[k0 : k0 + 1, :] * shifted_m
            + taps_ref[k0 + 3 : k0 + 4, :] * here
            + taps_ref[k0 + 6 : k0 + 7, :] * shifted_p
        )
        edge = jnp.where(inside, edge, 0.0)
        for r in range(16):
            x_scr[t, r // 8, j, r % 8] += jnp.where(sub == at, edge[r : r + 1], 0.0)

    conv_inner(1)

    def prepare(wqkv, load):
        load.wait()
        wk_scr[...] = wqkv[:, 512:1024]
        wqvt_scr[:512] = wqkv[:, :512].T
        wqvt_scr[512:] = wqkv[:, 1024:].T

    prepare(bqkv, loads[2])
    conv_inner(0)
    loads[1].wait()
    loads[3].wait()

    def send_out(i, unit, rows):
        pltpu.make_async_remote_copy(
            snd.at[i, unit, rows], rcv.at[i, me, rows], ssem.at[i], rsem.at[i],
            device_id=device_of(unit), device_id_type=MESH,
        ).start()

    def send_back(i, d):
        slot, device = peer(d)
        pltpu.make_async_remote_copy(
            snd2.at[i, slot], ret_ref.at[i, me], ssem2.at[i], rsem2.at[i],
            device_id=device, device_id_type=MESH,
        ).start()

    def all_of(t, src, dst, send, recv):
        return pltpu.make_async_remote_copy(
            src.at[t, pl.ds(0, PEERS - 1)], dst.at[t, pl.ds(0, PEERS - 1)], send.at[t], recv.at[t],
            device_id=(ri, ci), device_id_type=MESH,
        )

    def block(x_ref, normed, i, count, row):
        tokens = TOK * count

        def rounded():
            return x_ref[...].reshape(tokens, 512).astype(BF).astype(F32)

        if normed is None:
            normed = n_scr
            normed[...] = norm_rows(rounded(), bgain_ref[...])
        out = sublayer(tokens, normed, wk_scr, wqvt_scr, bwo, k_scr, qvt_scr, ot_scr) + rounded()
        for j in range(count):
            snd[i, :, pl.ds(row + 16 * j, 16), :] = to_planes(out[j * TOK : (j + 1) * TOK])
        rows = pl.ds(row, 16 * count)

        def start(d, c):
            send_out(i, lax.rem(me + d, PEERS), rows)
            return c

        lax.fori_loop(1, PEERS, start, 0, unroll=9)
        rcv[i, me, rows, :] = snd[i, me, rows, :]

    for half in range(2):
        x = x_scr[1, half].reshape(TOK, 512).astype(BF).astype(F32)
        n_mid[half] = norm_rows(x, bgain_ref[...])
    halo[0].wait_recv()
    halo[1].wait_recv()
    conv_outer(1)
    for half, r in ((0, 0), (1, 6)):
        x = x_scr[1, half, :, r : r + 2].reshape(64, 512).astype(BF).astype(F32)
        again = norm_rows(x, bgain_ref[...])
        for j in range(4):
            n_mid[half, 64 * j + 8 * r : 64 * j + 8 * r + 16, :] = again[16 * j : 16 * j + 16]

    def middle(i, carry):
        block(x_scr.at[1, i], n_mid.at[i], 0, 1, pl.multiple_of(16 * i, 16))
        return carry

    lax.fori_loop(0, 2, middle, 0)

    def sides(i, carry):
        @pl.when(i == 0)
        def _():
            halo[8].wait_recv()
            halo[9].wait_recv()
            conv_outer(0)
            conv_side(lcol, (3, 6, 7), ci > 0, 0, 0, 0, 0)

        @pl.when(i == 1)
        def _():
            halo[10].wait_recv()
            halo[11].wait_recv()
            conv_inner(2)
            conv_outer(2)
            conv_side(rcol, (2, 4, 5), ci < 7, 2, 3, 2, 7)

        block(x_scr.at[2 * i], None, 1 + i, 2, 0)
        return carry

    lax.fori_loop(0, 2, sides, 0)
    prepare(gqkv, loads[4])
    loads[5].wait()
    loads[6].wait()

    def own(i):
        return pltpu.make_async_copy(snd2.at[i, me], ret_ref.at[i, me], own_sem.at[i])

    def grid(i, carry):
        def place(q, lt):
            return pl.ds(16 * (q // 4) + 4 * lt + q % 4, PEERS, stride=32)

        all_of(i, snd, rcv, ssem, rsem).wait_recv()
        g_scr[...] = rcv[i].astype(F32).reshape(PEERS * 32, 128)
        for q in range(8):
            window = jnp.concatenate([g_scr[place(q, lt), :] for lt in range(4)], axis=1)
            n_scr[q * 64 : (q + 1) * 64] = norm_rows(window, ggain_ref[...])
        out = sublayer(2 * TOK, n_scr, wk_scr, wqvt_scr, gwo, k_scr, qvt_scr, ot_scr)
        for q in range(8):
            for lt in range(4):
                g_scr[place(q, lt), :] += out[q * 64 : (q + 1) * 64, lt * 128 : (lt + 1) * 128]
        snd2[i] = g_scr[...].reshape(PEERS, 32, 128).astype(BF)

        def start(d, c):
            send_back(i, d)
            return c

        lax.fori_loop(1, PEERS, start, 0, unroll=9)
        own(i).start()
        return carry

    lax.fori_loop(0, CHUNKS, grid, 0)

    for copy in halo:
        copy.wait_send()
    for t in range(CHUNKS):
        all_of(t, snd, rcv, ssem, rsem).wait_send()
    for t in range(CHUNKS):
        back = all_of(t, snd2, ret_ref, ssem2, rsem2)
        back.wait_send()
        back.wait_recv()
        own(t).wait()


def unpack_kernel(ret_ref, out_ref, frame, out_sem):
    leave = []
    for i, (t, half) in enumerate([(t, half) for t in (1, 0, 2) for half in range(2)]):
        y = from_planes(ret_ref[i // 2, :, 16 * half : 16 * half + 16, :]).reshape(4, 8, 8, 512)
        frame[i] = y.transpose(1, 0, 2, 3).reshape(8, 32, 512).astype(BF)
        place = out_ref.at[pl.ds(8 * half, 8), pl.ds(32 * t, 32)]
        leave.append(pltpu.make_async_copy(frame.at[i], place, out_sem.at[i]))
        leave[-1].start()
    for copy in leave:
        copy.wait()


def body(features, conv_taps, block_gain, block_qkv, block_out, grid_gain, grid_qkv, grid_out):
    any_ = pl.BlockSpec(memory_space=pl.ANY)
    vmem = pl.BlockSpec(memory_space=pltpu.VMEM)
    dma = pltpu.SemaphoreType.DMA
    planes = (CHUNKS, PEERS, 32, 128)
    returned = pl.pallas_call(
        main_kernel,
        out_shape=pltpu.VMEM(planes, BF),
        in_specs=[any_] * 8,
        out_specs=vmem,
        scratch_shapes=[
            pltpu.VMEM((9, 512), F32),
            pltpu.VMEM((1, 512), F32),
            pltpu.VMEM((1, 512), F32),
            pltpu.VMEM((18, 96, 512), BF),
            pltpu.VMEM((16, 512), BF),
            pltpu.VMEM((16, 512), BF),
            pltpu.VMEM((3, 16, 512), BF),
            pltpu.VMEM((3, 16, 512), BF),
            pltpu.VMEM((3, 2, 4, 8, 8, 512), F32),
            pltpu.VMEM((2 * PEERS * 16, 128), F32),
            pltpu.VMEM((512, 1536), BF),
            pltpu.VMEM((512, 1536), BF),
            pltpu.VMEM((512, 512), BF),
            pltpu.VMEM((512, 512), BF),
            pltpu.VMEM((512, 512), BF),
            pltpu.VMEM((1024, 512), BF),
            pltpu.VMEM((2 * TOK, 512), BF),
            pltpu.VMEM((2, TOK, 512), BF),
            pltpu.VMEM((2 * TOK, 512), BF),
            pltpu.VMEM((1024, 2 * TOK), BF),
            pltpu.VMEM((512, 2 * TOK), BF),
            pltpu.VMEM(planes, BF),
            pltpu.VMEM(planes, BF),
            pltpu.VMEM(planes, BF),
            dma((8,)),
            dma((12,)),
            dma((12,)),
            dma((CHUNKS,)),
            dma((CHUNKS,)),
            dma((CHUNKS,)),
            dma((CHUNKS,)),
            dma((CHUNKS,)),
        ],
        compiler_params=pltpu.CompilerParams(
            collective_id=0, has_side_effects=True, vmem_limit_bytes=60 * 2**20
        ),
    )(
        features, conv_taps, block_gain.reshape(1, 512), grid_gain.reshape(1, 512),
        block_qkv, block_out, grid_qkv, grid_out,
    )
    return pl.pallas_call(
        unpack_kernel,
        out_shape=jax.ShapeDtypeStruct(features.shape, BF),
        in_specs=[vmem],
        out_specs=any_,
        scratch_shapes=[
            pltpu.VMEM((2 * CHUNKS, 8, 32, 512), BF),
            dma((2 * CHUNKS,)),
        ],
        compiler_params=pltpu.CompilerParams(vmem_limit_bytes=16 * 2**20),
    )(returned)


def solution(mesh):
    placed = (P("rows", "cols", None), P(), P(), P(), P(), P(), P(), P())
    return jax.shard_map(
        body, mesh=mesh, in_specs=placed, out_specs=P("rows", "cols", None), check_vma=False
    )
```

```python
import jax
import jax.numpy as jnp
from jax import lax
from jax.experimental import pallas as pl
from jax.experimental.pallas import tpu as pltpu
from jax.sharding import PartitionSpec as P

MESH = pl.DeviceIdType.MESH
BF = jnp.bfloat16
F32 = jnp.float32
HEAD_DIM = 32
SCALE = HEAD_DIM ** -0.5
PEERS = 64
CHUNKS = 3
TOK = 256


def mm(a, b, dims=((1,), (0,))):
    return lax.dot_general(a, b, (dims, ((), ())), preferred_element_type=F32)


def norm_rows(x, gain):
    mean = jnp.mean(x, axis=-1, keepdims=True)
    cen = x - mean
    var = jnp.mean(cen * cen, axis=-1, keepdims=True)
    return (cen * lax.rsqrt(var + 1e-5) * gain).astype(BF)


def spread_heads(q):
    cols = []
    for h in range(4):
        parts = []
        if h > 0:
            parts.append(jnp.zeros((32 * h, 128), BF))
        parts.append(q[32 * h : 32 * (h + 1)])
        if h < 3:
            parts.append(jnp.zeros((32 * (3 - h), 128), BF))
        cols.append(jnp.concatenate(parts, axis=0))
    return jnp.concatenate(cols, axis=1)


def scores(unit, k_scr, qvt_scr):
    p, g = unit
    keys = k_scr[p * 128 : (p + 1) * 128, g * 128 : (g + 1) * 128]
    q = qvt_scr[g * 128 : (g + 1) * 128, p * 128 : (p + 1) * 128]
    s4 = mm(keys, spread_heads(q))
    first = lax.broadcasted_iota(jnp.int32, (64, 128), 1) < 64
    return [
        jnp.where(first, s4[:64, h * 128 : (h + 1) * 128], s4[64:, h * 128 : (h + 1) * 128])
        for h in range(4)
    ]


def soft(heads):
    lane = lax.broadcasted_iota(jnp.int32, (64, 128), 1)
    low = jnp.where(lane < 64, 1.0, 0.0).astype(BF)
    high = jnp.where(lane < 64, 0.0, 1.0).astype(BF)
    probs, inverse = [], []
    for s in heads:
        m = jnp.max(s, axis=0, keepdims=True)
        e = jnp.exp((s - m) * SCALE)
        inverse.append(1.0 / jnp.sum(e, axis=0, keepdims=True))
        pb = e.astype(BF)
        probs.append(jnp.concatenate([pb * low, pb * high], axis=0))
    return probs, inverse


def weigh(unit, softened, qvt_scr, ot_scr):
    p, g = unit
    probs, inverse = softened
    for h in range(0, 4, 2):
        r = g * 128 + h * 32
        v2 = qvt_scr[512 + r : 512 + r + 64, p * 128 : (p + 1) * 128]
        o2 = mm(v2, jnp.concatenate([probs[h], probs[h + 1]], axis=1))
        o = jnp.concatenate([o2[:32, :128] * inverse[h], o2[32:, 128:] * inverse[h + 1]], axis=0)
        ot_scr[r : r + 64, p * 128 : (p + 1) * 128] = o.astype(BF)


def sublayer(tokens, n_scr, wk_scr, wqvt_scr, wo_scr, k_scr, qvt_scr, ot_scr):
    tok = slice(0, tokens)
    normed = n_scr[tok]

    def project(first, size):
        rows = slice(first, first + size)
        qvt_scr[rows, tok] = mm(wqvt_scr[rows], normed, ((1,), (1,))).astype(BF)

    def keys(first):
        cols = slice(first, first + 256)
        k_scr[tok, cols] = mm(normed, wk_scr[:, cols]).astype(BF)

    pairs, b = tokens // 128, 2
    units = [(p, g) for half in range(2) for p in range(pairs) for g in (2 * half, 2 * half + 1)]
    n = len(units)
    keys(0)
    project(0, 256)
    ready = [scores(u, k_scr, qvt_scr) for u in units[:b]]
    project(512, 256)
    last, later = None, [lambda: keys(256), lambda: project(256, 256), lambda: project(768, 256)]
    out = None
    for i in range(0, n, b):
        now = ready
        if i // b >= n // (2 * b) - len(later) - 1:
            while later and i // b >= n // (2 * b) - len(later) - 1:
                later.pop(0)()
        if i + b < n:
            ready = [scores(u, k_scr, qvt_scr) for u in units[i + b : i + 2 * b]]
        done = [soft(s) for s in now]
        if last is not None:
            for u, x in zip(units[i - b : i], last):
                weigh(u, x, qvt_scr, ot_scr)
        last = done
        if i == n // 2 + b:
            out = mm(ot_scr[:256, tok], wo_scr[:256], ((0,), (0,)))
    for u, x in zip(units[n - b :], last):
        weigh(u, x, qvt_scr, ot_scr)
    return out + mm(ot_scr[256:, tok], wo_scr[256:], ((0,), (0,)))


def to_planes(x):
    y = x.reshape(32, 8, 512)
    upper = lax.broadcasted_iota(jnp.int32, (32, 8, 128), 1) < 4
    first, second = [], []
    for lt in range(0, 4, 2):
        a, b = y[:, :, lt * 128 : (lt + 1) * 128], y[:, :, (lt + 1) * 128 : (lt + 2) * 128]
        first.append(jnp.where(upper, a, pltpu.roll(b, 4, 1)))
        second.append(jnp.where(upper, pltpu.roll(a, 4, 1), b))
    halves = [jnp.concatenate(part, axis=1) for part in (first, second)]
    return jnp.concatenate(halves, axis=0).astype(BF)


def from_planes(planes):
    p = planes.astype(F32)
    upper = lax.broadcasted_iota(jnp.int32, (32, 8, 128), 1) < 4
    tiles = []
    for k in range(0, 16, 8):
        first, second = p[:32, k : k + 8], p[32:, k : k + 8]
        tiles.append(jnp.where(upper, first, pltpu.roll(second, 4, 1)))
        tiles.append(jnp.where(upper, pltpu.roll(first, 4, 1), second))
    return jnp.concatenate(tiles, axis=2)


def main_kernel(
    feat_ref, taps_hbm, bgain_hbm, ggain_hbm, bqkv_ref, bout_ref, gqkv_ref, gout_ref,
    ret_ref,
    taps_ref, bgain_ref, ggain_ref, fpad, coll, colr, lcol, rcol, x_scr, g_scr,
    bqkv, gqkv, bwo, gwo, wk_scr, wqvt_scr, n_scr, n_mid, k_scr, qvt_scr, ot_scr,
    snd, rcv, snd2,
    local_sem, halo_send, halo_recv, ssem, rsem, ssem2, rsem2, own_sem,
):
    ri, ci = lax.axis_index("rows"), lax.axis_index("cols")
    core = lax.rem(ri, 2)
    me = (ri // 2) * 8 + ci
    up, down = lax.rem(ri + 15, 16), lax.rem(ri + 1, 16)
    left, right = lax.rem(ci + 7, 8), lax.rem(ci + 1, 8)

    def device_of(unit):
        return 2 * (unit // 8) + core, lax.rem(unit, 8)

    def peer(d):
        unit = lax.rem(me + d, PEERS)
        return unit, device_of(unit)

    barrier = pltpu.get_barrier_semaphore()

    def greet(d, carry):
        pl.semaphore_signal(barrier, inc=1, device_id=peer(d)[1], device_id_type=MESH)
        return carry

    load_edge = [
        pltpu.make_async_copy(feat_ref.at[r], fpad.at[r + 1], local_sem.at[8 + i]) for i, r in enumerate((0, 15))
    ]
    load_feat = pltpu.make_async_copy(feat_ref.at[pl.ds(1, 14)], fpad.at[pl.ds(2, 14)], local_sem.at[0])
    for load in load_edge:
        load.start()
    load_feat.start()
    lax.fori_loop(1, PEERS, greet, 0, unroll=9)
    around = [(r, c) for r in (up, down) for c in (left, ci, right)]
    for r, c in around:
        pl.semaphore_signal(barrier, inc=1, device_id=(r, c), device_id_type=MESH)
    loads = [
        pltpu.make_async_copy(src, dst, local_sem.at[i + 1])
        for i, (src, dst) in enumerate(
            (
                (taps_hbm, taps_ref), (bgain_hbm, bgain_ref), (bqkv_ref, bqkv), (bout_ref, bwo),
                (gqkv_ref, gqkv), (gout_ref, gwo), (ggain_hbm, ggain_ref),
            )
        )
    ]
    for load in loads:
        load.start()

    for load in load_edge:
        load.wait()
    pl.semaphore_wait(barrier, PEERS - 1 + len(around))

    halo = [
        (fpad.at[1, pl.ds(16, 64)], fpad.at[17, pl.ds(16, 64)], (up, ci)),
        (fpad.at[16, pl.ds(16, 64)], fpad.at[0, pl.ds(16, 64)], (down, ci)),
        (coll, rcol.at[1], (ri, left)),
        (colr, lcol.at[1], (ri, right)),
        (coll, rcol.at[2], (up, left)),
        (coll, rcol.at[0], (down, left)),
        (colr, lcol.at[2], (up, right)),
        (colr, lcol.at[0], (down, right)),
        (fpad.at[1, pl.ds(0, 16)], fpad.at[17, pl.ds(0, 16)], (up, ci)),
        (fpad.at[16, pl.ds(0, 16)], fpad.at[0, pl.ds(0, 16)], (down, ci)),
        (fpad.at[1, pl.ds(80, 16)], fpad.at[17, pl.ds(80, 16)], (up, ci)),
        (fpad.at[16, pl.ds(80, 16)], fpad.at[0, pl.ds(80, 16)], (down, ci)),
    ]
    halo = [
        pltpu.make_async_remote_copy(
            src, dst, halo_send.at[i], halo_recv.at[i], device_id=to, device_id_type=MESH
        )
        for i, (src, dst, to) in enumerate(halo)
    ]
    for copy in halo[:2]:
        copy.start()
    load_feat.wait()
    loads[0].wait()
    for r in range(16):
        coll[r : r + 1, :] = fpad[r + 1, 0:1, :]
        colr[r : r + 1, :] = fpad[r + 1, 95:96, :]
    for copy in halo[2:]:
        copy.start()
    not_top, not_bottom = ri > 0, ri < 15

    def conv_row(t, r, above, below):
        half, rr = r // 8, lax.rem(r, 8)
        c0 = 32 * t
        lo, hi = max(c0 - 16, 0), min(c0 + 48, 96)
        pre, post = 8 * (t > 0), 8 * (t < 2)
        for lt in range(4):
            lanes = slice(lt * 128, (lt + 1) * 128)
            xm = fpad[r, lo:hi, lanes].astype(F32)
            x0 = fpad[r + 1, lo:hi, lanes].astype(F32)
            xp = fpad[r + 2, lo:hi, lanes].astype(F32)
            if above is not None:
                xm = jnp.where(above, xm, 0.0)
            if below is not None:
                xp = jnp.where(below, xp, 0.0)

            def column(j, start, stop):
                k = slice(start - lo, stop - lo)
                tap = [taps_ref[i : i + 1, lanes] for i in (j, j + 3, j + 6)]
                return tap[0] * xm[k] + tap[1] * x0[k] + tap[2] * xp[k]

            a0 = pltpu.roll(column(0, c0 - pre, c0 + 32), 1, 0)
            a1 = column(1, c0, c0 + 32)
            a2 = pltpu.roll(column(2, c0, c0 + 32 + post), 31 + post, 0)
            row = lax.broadcasted_iota(jnp.int32, (32, 128), 0)
            a0 = a0[8:] if pre else jnp.where(row == 0, 0.0, a0)
            a2 = a2[:32] if post else jnp.where(row == 31, 0.0, a2)
            y = x0[c0 - lo : c0 - lo + 32] + a1 + a0 + a2
            x_scr[t, half, :, rr, :, lanes] = y.reshape(4, 8, 128)

    def conv_inner(t):
        def inner(r, carry):
            conv_row(t, r, None, None)
            return carry

        lax.fori_loop(1, 15, inner, 0)

    def conv_outer(t):
        conv_row(t, 0, not_top, None)
        conv_row(t, 15, None, not_bottom)

    def conv_side(cols, arrivals, inside, k0, j, t, at):
        for i in arrivals:
            halo[i].wait_recv()
        row_of = lax.broadcasted_iota(jnp.int32, (16, 512), 0)
        sub = lax.broadcasted_iota(jnp.int32, (8, 512), 0)
        here = cols[1].astype(F32)
        before = jnp.where(not_top, cols[0].astype(F32)[15:16], 0.0)
        after = jnp.where(not_bottom, cols[2].astype(F32)[0:1], 0.0)
        shifted_m = jnp.where(row_of == 0, before, pltpu.roll(here, 1, 0))
        shifted_p = jnp.where(row_of == 15, after, pltpu.roll(here, 15, 0))
        edge = (
            taps_ref[k0 : k0 + 1, :] * shifted_m
            + taps_ref[k0 + 3 : k0 + 4, :] * here
            + taps_ref[k0 + 6 : k0 + 7, :] * shifted_p
        )
        edge = jnp.where(inside, edge, 0.0)
        for r in range(16):
            x_scr[t, r // 8, j, r % 8] += jnp.where(sub == at, edge[r : r + 1], 0.0)

    conv_inner(1)

    def prepare(wqkv, load):
        load.wait()
        wk_scr[...] = wqkv[:, 512:1024]
        wqvt_scr[:512] = wqkv[:, :512].T
        wqvt_scr[512:] = wqkv[:, 1024:].T

    prepare(bqkv, loads[2])
    conv_inner(0)
    loads[1].wait()
    loads[3].wait()

    def send_out(i, unit, rows):
        pltpu.make_async_remote_copy(
            snd.at[i, unit, rows], rcv.at[i, me, rows], ssem.at[i], rsem.at[i],
            device_id=device_of(unit), device_id_type=MESH,
        ).start()

    def send_back(i, d):
        slot, device = peer(d)
        pltpu.make_async_remote_copy(
            snd2.at[i, slot], ret_ref.at[i, me], ssem2.at[i], rsem2.at[i],
            device_id=device, device_id_type=MESH,
        ).start()

    def all_of(t, src, dst, send, recv):
        return pltpu.make_async_remote_copy(
            src.at[t, pl.ds(0, PEERS - 1)], dst.at[t, pl.ds(0, PEERS - 1)], send.at[t], recv.at[t],
            device_id=(ri, ci), device_id_type=MESH,
        )

    def block(x_ref, normed, i, count, row):
        tokens = TOK * count

        def rounded():
            return x_ref[...].reshape(tokens, 512).astype(BF).astype(F32)

        if normed is None:
            normed = n_scr
            normed[...] = norm_rows(rounded(), bgain_ref[...])
        out = sublayer(tokens, normed, wk_scr, wqvt_scr, bwo, k_scr, qvt_scr, ot_scr) + rounded()
        for j in range(count):
            snd[i, :, pl.ds(row + 16 * j, 16), :] = to_planes(out[j * TOK : (j + 1) * TOK])
        rows = pl.ds(row, 16 * count)

        def start(d, c):
            send_out(i, lax.rem(me + d, PEERS), rows)
            return c

        lax.fori_loop(1, PEERS, start, 0, unroll=9)
        rcv[i, me, rows, :] = snd[i, me, rows, :]

    for half in range(2):
        x = x_scr[1, half].reshape(TOK, 512).astype(BF).astype(F32)
        n_mid[half] = norm_rows(x, bgain_ref[...])

    def norm_again(half, r):
        x = x_scr[1, half, :, r : r + 2].reshape(64, 512).astype(BF).astype(F32)
        again = norm_rows(x, bgain_ref[...])
        for j in range(4):
            n_mid[half, 64 * j + 8 * r : 64 * j + 8 * r + 16, :] = again[16 * j : 16 * j + 16]


    def middle(i, carry):
        @pl.when(i == 0)
        def _():
            halo[1].wait_recv()
            conv_row(1, 0, not_top, None)
            norm_again(0, 0)

        @pl.when(i == 1)
        def _():
            halo[0].wait_recv()
            conv_row(1, 15, None, not_bottom)
            norm_again(1, 6)

        block(x_scr.at[1, i], n_mid.at[i], 0, 1, pl.multiple_of(16 * i, 16))
        return carry

    lax.fori_loop(0, 2, middle, 0)

    def sides(i, carry):
        @pl.when(i == 0)
        def _():
            halo[8].wait_recv()
            halo[9].wait_recv()
            conv_outer(0)
            conv_side(lcol, (3, 6, 7), ci > 0, 0, 0, 0, 0)

        @pl.when(i == 1)
        def _():
            halo[10].wait_recv()
            halo[11].wait_recv()
            conv_inner(2)
            conv_outer(2)
            conv_side(rcol, (2, 4, 5), ci < 7, 2, 3, 2, 7)

        block(x_scr.at[2 * i], None, 1 + i, 2, 0)
        return carry

    lax.fori_loop(0, 2, sides, 0)
    prepare(gqkv, loads[4])
    loads[5].wait()
    loads[6].wait()

    def own(i):
        return pltpu.make_async_copy(snd2.at[i, me], ret_ref.at[i, me], own_sem.at[i])

    def grid(i, carry):
        def place(q, lt):
            return pl.ds(16 * (q // 4) + 4 * lt + q % 4, PEERS, stride=32)

        all_of(i, snd, rcv, ssem, rsem).wait_recv()
        g_scr[...] = rcv[i].astype(F32).reshape(PEERS * 32, 128)
        for q in range(8):
            window = jnp.concatenate([g_scr[place(q, lt), :] for lt in range(4)], axis=1)
            n_scr[q * 64 : (q + 1) * 64] = norm_rows(window, ggain_ref[...])
        out = sublayer(2 * TOK, n_scr, wk_scr, wqvt_scr, gwo, k_scr, qvt_scr, ot_scr)
        for q in range(8):
            for lt in range(4):
                g_scr[place(q, lt), :] += out[q * 64 : (q + 1) * 64, lt * 128 : (lt + 1) * 128]
        snd2[i] = g_scr[...].reshape(PEERS, 32, 128).astype(BF)

        def start(d, c):
            send_back(i, d)
            return c

        lax.fori_loop(1, PEERS, start, 0, unroll=9)
        own(i).start()
        return carry

    lax.fori_loop(0, CHUNKS, grid, 0)

    for copy in halo:
        copy.wait_send()
    for t in range(CHUNKS):
        all_of(t, snd, rcv, ssem, rsem).wait_send()
    for t in range(CHUNKS):
        back = all_of(t, snd2, ret_ref, ssem2, rsem2)
        back.wait_send()
        back.wait_recv()
        own(t).wait()


def unpack_kernel(ret_ref, out_ref, frame, out_sem):
    leave = []
    for i, (t, half) in enumerate([(t, half) for t in (1, 0, 2) for half in range(2)]):
        y = from_planes(ret_ref[i // 2, :, 16 * half : 16 * half + 16, :]).reshape(4, 8, 8, 512)
        frame[i] = y.transpose(1, 0, 2, 3).reshape(8, 32, 512).astype(BF)
        place = out_ref.at[pl.ds(8 * half, 8), pl.ds(32 * t, 32)]
        leave.append(pltpu.make_async_copy(frame.at[i], place, out_sem.at[i]))
        leave[-1].start()
    for copy in leave:
        copy.wait()


def body(features, conv_taps, block_gain, block_qkv, block_out, grid_gain, grid_qkv, grid_out):
    any_ = pl.BlockSpec(memory_space=pl.ANY)
    vmem = pl.BlockSpec(memory_space=pltpu.VMEM)
    dma = pltpu.SemaphoreType.DMA
    planes = (CHUNKS, PEERS, 32, 128)
    returned = pl.pallas_call(
        main_kernel,
        out_shape=pltpu.VMEM(planes, BF),
        in_specs=[any_] * 8,
        out_specs=vmem,
        scratch_shapes=[
            pltpu.VMEM((9, 512), F32),
            pltpu.VMEM((1, 512), F32),
            pltpu.VMEM((1, 512), F32),
            pltpu.VMEM((18, 96, 512), BF),
            pltpu.VMEM((16, 512), BF),
            pltpu.VMEM((16, 512), BF),
            pltpu.VMEM((3, 16, 512), BF),
            pltpu.VMEM((3, 16, 512), BF),
            pltpu.VMEM((3, 2, 4, 8, 8, 512), F32),
            pltpu.VMEM((2 * PEERS * 16, 128), F32),
            pltpu.VMEM((512, 1536), BF),
            pltpu.VMEM((512, 1536), BF),
            pltpu.VMEM((512, 512), BF),
            pltpu.VMEM((512, 512), BF),
            pltpu.VMEM((512, 512), BF),
            pltpu.VMEM((1024, 512), BF),
            pltpu.VMEM((2 * TOK, 512), BF),
            pltpu.VMEM((2, TOK, 512), BF),
            pltpu.VMEM((2 * TOK, 512), BF),
            pltpu.VMEM((1024, 2 * TOK), BF),
            pltpu.VMEM((512, 2 * TOK), BF),
            pltpu.VMEM(planes, BF),
            pltpu.VMEM(planes, BF),
            pltpu.VMEM(planes, BF),
            dma((10,)),
            dma((12,)),
            dma((12,)),
            dma((CHUNKS,)),
            dma((CHUNKS,)),
            dma((CHUNKS,)),
            dma((CHUNKS,)),
            dma((CHUNKS,)),
        ],
        compiler_params=pltpu.CompilerParams(
            collective_id=0, has_side_effects=True, vmem_limit_bytes=60 * 2**20
        ),
    )(
        features, conv_taps, block_gain.reshape(1, 512), grid_gain.reshape(1, 512),
        block_qkv, block_out, grid_qkv, grid_out,
    )
    return pl.pallas_call(
        unpack_kernel,
        out_shape=jax.ShapeDtypeStruct(features.shape, BF),
        in_specs=[vmem],
        out_specs=any_,
        scratch_shapes=[
            pltpu.VMEM((2 * CHUNKS, 8, 32, 512), BF),
            dma((2 * CHUNKS,)),
        ],
        compiler_params=pltpu.CompilerParams(vmem_limit_bytes=16 * 2**20),
    )(returned)


def solution(mesh):
    placed = (P("rows", "cols", None), P(), P(), P(), P(), P(), P(), P())
    return jax.shard_map(
        body, mesh=mesh, in_specs=placed, out_specs=P("rows", "cols", None), check_vma=False
    )
```

```python
import jax
import jax.numpy as jnp
from jax import lax
from jax.experimental import pallas as pl
from jax.experimental.pallas import tpu as pltpu
from jax.sharding import PartitionSpec as P

MESH = pl.DeviceIdType.MESH
BF = jnp.bfloat16
F32 = jnp.float32
HEAD_DIM = 32
SCALE = HEAD_DIM ** -0.5
PEERS = 64
CHUNKS = 3
TOK = 256


def mm(a, b, dims=((1,), (0,))):
    return lax.dot_general(a, b, (dims, ((), ())), preferred_element_type=F32)


def norm_rows(x, gain):
    mean = jnp.mean(x, axis=-1, keepdims=True)
    cen = x - mean
    var = jnp.mean(cen * cen, axis=-1, keepdims=True)
    return (cen * lax.rsqrt(var + 1e-5) * gain).astype(BF)


def spread_heads(q):
    cols = []
    for h in range(4):
        parts = []
        if h > 0:
            parts.append(jnp.zeros((32 * h, 128), BF))
        parts.append(q[32 * h : 32 * (h + 1)])
        if h < 3:
            parts.append(jnp.zeros((32 * (3 - h), 128), BF))
        cols.append(jnp.concatenate(parts, axis=0))
    return jnp.concatenate(cols, axis=1)


def scores(unit, k_scr, qvt_scr):
    p, g = unit
    keys = k_scr[p * 128 : (p + 1) * 128, g * 128 : (g + 1) * 128]
    q = qvt_scr[g * 128 : (g + 1) * 128, p * 128 : (p + 1) * 128]
    s4 = mm(keys, spread_heads(q))
    first = lax.broadcasted_iota(jnp.int32, (64, 128), 1) < 64
    return [
        jnp.where(first, s4[:64, h * 128 : (h + 1) * 128], s4[64:, h * 128 : (h + 1) * 128])
        for h in range(4)
    ]


def soft(heads):
    lane = lax.broadcasted_iota(jnp.int32, (64, 128), 1)
    low = jnp.where(lane < 64, 1.0, 0.0).astype(BF)
    high = jnp.where(lane < 64, 0.0, 1.0).astype(BF)
    probs, inverse = [], []
    for s in heads:
        m = jnp.max(s, axis=0, keepdims=True)
        e = jnp.exp((s - m) * SCALE)
        inverse.append(1.0 / jnp.sum(e, axis=0, keepdims=True))
        pb = e.astype(BF)
        probs.append(jnp.concatenate([pb * low, pb * high], axis=0))
    return probs, inverse


def weigh(unit, softened, qvt_scr, ot_scr):
    p, g = unit
    probs, inverse = softened
    for h in range(0, 4, 2):
        r = g * 128 + h * 32
        v2 = qvt_scr[512 + r : 512 + r + 64, p * 128 : (p + 1) * 128]
        o2 = mm(v2, jnp.concatenate([probs[h], probs[h + 1]], axis=1))
        o = jnp.concatenate([o2[:32, :128] * inverse[h], o2[32:, 128:] * inverse[h + 1]], axis=0)
        ot_scr[r : r + 64, p * 128 : (p + 1) * 128] = o.astype(BF)


def attend(pairs, k_scr, qvt_scr, ot_scr):
    units = [(p, g) for p in range(pairs) for g in range(4)]
    n, b = len(units), 2
    ready = [scores(u, k_scr, qvt_scr) for u in units[:b]]
    last = None
    for i in range(0, n, b):
        now = ready
        if i + b < n:
            ready = [scores(u, k_scr, qvt_scr) for u in units[i + b : i + 2 * b]]
        done = [soft(s) for s in now]
        if last is not None:
            for u, x in zip(units[i - b : i], last):
                weigh(u, x, qvt_scr, ot_scr)
        last = done
    for u, x in zip(units[n - b :], last):
        weigh(u, x, qvt_scr, ot_scr)


def sublayer_whole(tokens, n_scr, wk_scr, wqvt_scr, wo_scr, k_scr, qvt_scr, ot_scr):
    normed = n_scr[:tokens]
    k_scr[:tokens] = mm(normed, wk_scr[...]).astype(BF)
    qvt_scr[:, :tokens] = mm(wqvt_scr[...], normed, ((1,), (1,))).astype(BF)
    attend(tokens // 128, k_scr, qvt_scr, ot_scr)
    return mm(ot_scr[:, :tokens], wo_scr[...], ((0,), (0,)))


def sublayer(tokens, n_scr, wk_scr, wqvt_scr, wo_scr, k_scr, qvt_scr, ot_scr):
    tok = slice(0, tokens)
    normed = n_scr[tok]

    def project(first, size):
        rows = slice(first, first + size)
        qvt_scr[rows, tok] = mm(wqvt_scr[rows], normed, ((1,), (1,))).astype(BF)

    def keys(first):
        cols = slice(first, first + 256)
        k_scr[tok, cols] = mm(normed, wk_scr[:, cols]).astype(BF)

    pairs, b = tokens // 128, 2
    units = [(p, g) for half in range(2) for p in range(pairs) for g in (2 * half, 2 * half + 1)]
    n = len(units)
    keys(0)
    project(0, 256)
    ready = [scores(u, k_scr, qvt_scr) for u in units[:b]]
    project(512, 256)
    last, later = None, [lambda: keys(256), lambda: project(256, 256), lambda: project(768, 256)]
    out = None
    for i in range(0, n, b):
        now = ready
        if i // b >= n // (2 * b) - len(later) - 1:
            while later and i // b >= n // (2 * b) - len(later) - 1:
                later.pop(0)()
        if i + b < n:
            ready = [scores(u, k_scr, qvt_scr) for u in units[i + b : i + 2 * b]]
        done = [soft(s) for s in now]
        if last is not None:
            for u, x in zip(units[i - b : i], last):
                weigh(u, x, qvt_scr, ot_scr)
        last = done
        if i == n // 2 + b:
            out = mm(ot_scr[:256, tok], wo_scr[:256], ((0,), (0,)))
    for u, x in zip(units[n - b :], last):
        weigh(u, x, qvt_scr, ot_scr)
    return out + mm(ot_scr[256:, tok], wo_scr[256:], ((0,), (0,)))


def to_planes(x):
    y = x.reshape(32, 8, 512)
    upper = lax.broadcasted_iota(jnp.int32, (32, 8, 128), 1) < 4
    first, second = [], []
    for lt in range(0, 4, 2):
        a, b = y[:, :, lt * 128 : (lt + 1) * 128], y[:, :, (lt + 1) * 128 : (lt + 2) * 128]
        first.append(jnp.where(upper, a, pltpu.roll(b, 4, 1)))
        second.append(jnp.where(upper, pltpu.roll(a, 4, 1), b))
    halves = [jnp.concatenate(part, axis=1) for part in (first, second)]
    return jnp.concatenate(halves, axis=0).astype(BF)


def from_planes(planes):
    p = planes.astype(F32)
    upper = lax.broadcasted_iota(jnp.int32, (32, 8, 128), 1) < 4
    tiles = []
    for k in range(0, 16, 8):
        first, second = p[:32, k : k + 8], p[32:, k : k + 8]
        tiles.append(jnp.where(upper, first, pltpu.roll(second, 4, 1)))
        tiles.append(jnp.where(upper, pltpu.roll(first, 4, 1), second))
    return jnp.concatenate(tiles, axis=2)


def main_kernel(
    feat_ref, taps_hbm, bgain_hbm, ggain_hbm, bqkv_ref, bout_ref, gqkv_ref, gout_ref,
    ret_ref,
    taps_ref, bgain_ref, ggain_ref, fpad, coll, colr, lcol, rcol, x_scr, g_scr,
    bqkv, gqkv, bwo, gwo, wk_scr, wqvt_scr, n_scr, n_mid, k_scr, qvt_scr, ot_scr,
    snd, rcv, snd2,
    local_sem, halo_send, halo_recv, ssem, rsem, ssem2, rsem2, own_sem,
):
    ri, ci = lax.axis_index("rows"), lax.axis_index("cols")
    core = lax.rem(ri, 2)
    me = (ri // 2) * 8 + ci
    up, down = lax.rem(ri + 15, 16), lax.rem(ri + 1, 16)
    left, right = lax.rem(ci + 7, 8), lax.rem(ci + 1, 8)

    def device_of(unit):
        return 2 * (unit // 8) + core, lax.rem(unit, 8)

    def peer(d):
        unit = lax.rem(me + d, PEERS)
        return unit, device_of(unit)

    barrier = pltpu.get_barrier_semaphore()

    def greet(d, carry):
        pl.semaphore_signal(barrier, inc=1, device_id=peer(d)[1], device_id_type=MESH)
        return carry

    load_edge = [
        pltpu.make_async_copy(feat_ref.at[r], fpad.at[r + 1], local_sem.at[8 + i]) for i, r in enumerate((0, 15))
    ]
    load_feat = pltpu.make_async_copy(feat_ref.at[pl.ds(1, 14)], fpad.at[pl.ds(2, 14)], local_sem.at[0])
    for load in load_edge:
        load.start()
    load_feat.start()
    lax.fori_loop(1, PEERS, greet, 0, unroll=9)
    around = [(r, c) for r in (up, down) for c in (left, ci, right)]
    for r, c in around:
        pl.semaphore_signal(barrier, inc=1, device_id=(r, c), device_id_type=MESH)
    loads = [
        pltpu.make_async_copy(src, dst, local_sem.at[i + 1])
        for i, (src, dst) in enumerate(
            (
                (taps_hbm, taps_ref), (bgain_hbm, bgain_ref), (bqkv_ref, bqkv), (bout_ref, bwo),
                (gqkv_ref, gqkv), (gout_ref, gwo), (ggain_hbm, ggain_ref),
            )
        )
    ]
    for load in loads:
        load.start()

    for load in load_edge:
        load.wait()
    pl.semaphore_wait(barrier, PEERS - 1 + len(around))

    halo = [
        (fpad.at[1, pl.ds(16, 64)], fpad.at[17, pl.ds(16, 64)], (up, ci)),
        (fpad.at[16, pl.ds(16, 64)], fpad.at[0, pl.ds(16, 64)], (down, ci)),
        (coll, rcol.at[1], (ri, left)),
        (colr, lcol.at[1], (ri, right)),
        (coll, rcol.at[2], (up, left)),
        (coll, rcol.at[0], (down, left)),
        (colr, lcol.at[2], (up, right)),
        (colr, lcol.at[0], (down, right)),
        (fpad.at[1, pl.ds(0, 16)], fpad.at[17, pl.ds(0, 16)], (up, ci)),
        (fpad.at[16, pl.ds(0, 16)], fpad.at[0, pl.ds(0, 16)], (down, ci)),
        (fpad.at[1, pl.ds(80, 16)], fpad.at[17, pl.ds(80, 16)], (up, ci)),
        (fpad.at[16, pl.ds(80, 16)], fpad.at[0, pl.ds(80, 16)], (down, ci)),
    ]
    halo = [
        pltpu.make_async_remote_copy(
            src, dst, halo_send.at[i], halo_recv.at[i], device_id=to, device_id_type=MESH
        )
        for i, (src, dst, to) in enumerate(halo)
    ]
    halo[1].start()
    halo[0].start()
    load_feat.wait()
    loads[0].wait()
    for r in range(16):
        coll[r : r + 1, :] = fpad[r + 1, 0:1, :]
        colr[r : r + 1, :] = fpad[r + 1, 95:96, :]
    for copy in halo[2:]:
        copy.start()
    not_top, not_bottom = ri > 0, ri < 15

    def conv_row(t, r, above, below):
        half, rr = r // 8, lax.rem(r, 8)
        c0 = 32 * t
        lo, hi = max(c0 - 16, 0), min(c0 + 48, 96)
        pre, post = 8 * (t > 0), 8 * (t < 2)
        for lt in range(4):
            lanes = slice(lt * 128, (lt + 1) * 128)
            xm = fpad[r, lo:hi, lanes].astype(F32)
            x0 = fpad[r + 1, lo:hi, lanes].astype(F32)
            xp = fpad[r + 2, lo:hi, lanes].astype(F32)
            if above is not None:
                xm = jnp.where(above, xm, 0.0)
            if below is not None:
                xp = jnp.where(below, xp, 0.0)

            def column(j, start, stop):
                k = slice(start - lo, stop - lo)
                tap = [taps_ref[i : i + 1, lanes] for i in (j, j + 3, j + 6)]
                return tap[0] * xm[k] + tap[1] * x0[k] + tap[2] * xp[k]

            a0 = pltpu.roll(column(0, c0 - pre, c0 + 32), 1, 0)
            a1 = column(1, c0, c0 + 32)
            a2 = pltpu.roll(column(2, c0, c0 + 32 + post), 31 + post, 0)
            row = lax.broadcasted_iota(jnp.int32, (32, 128), 0)
            a0 = a0[8:] if pre else jnp.where(row == 0, 0.0, a0)
            a2 = a2[:32] if post else jnp.where(row == 31, 0.0, a2)
            y = x0[c0 - lo : c0 - lo + 32] + a1 + a0 + a2
            x_scr[t, half, :, rr, :, lanes] = y.reshape(4, 8, 128)

    def conv_inner(t):
        def inner(r, carry):
            conv_row(t, r, None, None)
            return carry

        lax.fori_loop(1, 15, inner, 0)

    def conv_outer(t):
        conv_row(t, 0, not_top, None)
        conv_row(t, 15, None, not_bottom)

    def conv_side(cols, arrivals, inside, k0, j, t, at):
        for i in arrivals:
            halo[i].wait_recv()
        row_of = lax.broadcasted_iota(jnp.int32, (16, 512), 0)
        sub = lax.broadcasted_iota(jnp.int32, (8, 512), 0)
        here = cols[1].astype(F32)
        before = jnp.where(not_top, cols[0].astype(F32)[15:16], 0.0)
        after = jnp.where(not_bottom, cols[2].astype(F32)[0:1], 0.0)
        shifted_m = jnp.where(row_of == 0, before, pltpu.roll(here, 1, 0))
        shifted_p = jnp.where(row_of == 15, after, pltpu.roll(here, 15, 0))
        edge = (
            taps_ref[k0 : k0 + 1, :] * shifted_m
            + taps_ref[k0 + 3 : k0 + 4, :] * here
            + taps_ref[k0 + 6 : k0 + 7, :] * shifted_p
        )
        edge = jnp.where(inside, edge, 0.0)
        for r in range(16):
            x_scr[t, r // 8, j, r % 8] += jnp.where(sub == at, edge[r : r + 1], 0.0)

    conv_inner(1)

    def prepare(wqkv, load):
        load.wait()
        wk_scr[...] = wqkv[:, 512:1024]
        wqvt_scr[:512] = wqkv[:, :512].T
        wqvt_scr[512:] = wqkv[:, 1024:].T

    prepare(bqkv, loads[2])
    conv_inner(0)
    loads[1].wait()
    loads[3].wait()

    def send_out(i, unit, rows):
        pltpu.make_async_remote_copy(
            snd.at[i, unit, rows], rcv.at[i, me, rows], ssem.at[i], rsem.at[i],
            device_id=device_of(unit), device_id_type=MESH,
        ).start()

    def send_back(i, d):
        slot, device = peer(d)
        pltpu.make_async_remote_copy(
            snd2.at[i, slot], ret_ref.at[i, me], ssem2.at[i], rsem2.at[i],
            device_id=device, device_id_type=MESH,
        ).start()

    def all_of(t, src, dst, send, recv):
        return pltpu.make_async_remote_copy(
            src.at[t, pl.ds(0, PEERS - 1)], dst.at[t, pl.ds(0, PEERS - 1)], send.at[t], recv.at[t],
            device_id=(ri, ci), device_id_type=MESH,
        )

    def block(x_ref, normed, i, count, row):
        tokens = TOK * count

        def rounded():
            return x_ref[...].reshape(tokens, 512).astype(BF).astype(F32)

        if normed is None:
            normed = n_scr
            normed[...] = norm_rows(rounded(), bgain_ref[...])
        apply = sublayer if count == 1 else sublayer_whole
        out = apply(tokens, normed, wk_scr, wqvt_scr, bwo, k_scr, qvt_scr, ot_scr) + rounded()
        for j in range(count):
            snd[i, :, pl.ds(row + 16 * j, 16), :] = to_planes(out[j * TOK : (j + 1) * TOK])
        rows = pl.ds(row, 16 * count)

        def start(d, c):
            send_out(i, lax.rem(me + d, PEERS), rows)
            return c

        lax.fori_loop(1, PEERS, start, 0, unroll=9)
        rcv[i, me, rows, :] = snd[i, me, rows, :]

    for half in range(2):
        x = x_scr[1, half].reshape(TOK, 512).astype(BF).astype(F32)
        n_mid[half] = norm_rows(x, bgain_ref[...])

    def norm_again(half, r):
        x = x_scr[1, half, :, r : r + 2].reshape(64, 512).astype(BF).astype(F32)
        again = norm_rows(x, bgain_ref[...])
        for j in range(4):
            n_mid[half, 64 * j + 8 * r : 64 * j + 8 * r + 16, :] = again[16 * j : 16 * j + 16]


    def middle(i, carry):
        @pl.when(i == 0)
        def _():
            halo[1].wait_recv()
            conv_row(1, 0, not_top, None)
            norm_again(0, 0)

        @pl.when(i == 1)
        def _():
            halo[0].wait_recv()
            conv_row(1, 15, None, not_bottom)
            norm_again(1, 6)

        block(x_scr.at[1, i], n_mid.at[i], 0, 1, pl.multiple_of(16 * i, 16))
        return carry

    lax.fori_loop(0, 2, middle, 0)

    def sides(i, carry):
        @pl.when(i == 0)
        def _():
            halo[8].wait_recv()
            halo[9].wait_recv()
            conv_outer(0)
            conv_side(lcol, (3, 6, 7), ci > 0, 0, 0, 0, 0)

        @pl.when(i == 1)
        def _():
            halo[10].wait_recv()
            halo[11].wait_recv()
            conv_inner(2)
            conv_outer(2)
            conv_side(rcol, (2, 4, 5), ci < 7, 2, 3, 2, 7)

        block(x_scr.at[2 * i], None, 1 + i, 2, 0)
        return carry

    lax.fori_loop(0, 2, sides, 0)
    prepare(gqkv, loads[4])
    loads[5].wait()
    loads[6].wait()

    def own(i):
        return pltpu.make_async_copy(snd2.at[i, me], ret_ref.at[i, me], own_sem.at[i])

    def grid(i, carry):
        def place(q, lt):
            return pl.ds(16 * (q // 4) + 4 * lt + q % 4, PEERS, stride=32)

        all_of(i, snd, rcv, ssem, rsem).wait_recv()
        g_scr[...] = rcv[i].astype(F32).reshape(PEERS * 32, 128)
        for q in range(8):
            window = jnp.concatenate([g_scr[place(q, lt), :] for lt in range(4)], axis=1)
            n_scr[q * 64 : (q + 1) * 64] = norm_rows(window, ggain_ref[...])
        out = sublayer_whole(2 * TOK, n_scr, wk_scr, wqvt_scr, gwo, k_scr, qvt_scr, ot_scr)
        for q in range(8):
            for lt in range(4):
                g_scr[place(q, lt), :] += out[q * 64 : (q + 1) * 64, lt * 128 : (lt + 1) * 128]
        snd2[i] = g_scr[...].reshape(PEERS, 32, 128).astype(BF)

        def start(d, c):
            send_back(i, d)
            return c

        lax.fori_loop(1, PEERS, start, 0, unroll=9)
        own(i).start()
        return carry

    lax.fori_loop(0, CHUNKS, grid, 0)

    for copy in halo:
        copy.wait_send()
    for t in range(CHUNKS):
        all_of(t, snd, rcv, ssem, rsem).wait_send()
    for t in range(CHUNKS):
        back = all_of(t, snd2, ret_ref, ssem2, rsem2)
        back.wait_send()
        back.wait_recv()
        own(t).wait()


def unpack_kernel(ret_ref, out_ref, frame, out_sem):
    leave = []
    for i, (t, half) in enumerate([(t, half) for t in (1, 0, 2) for half in range(2)]):
        y = from_planes(ret_ref[i // 2, :, 16 * half : 16 * half + 16, :]).reshape(4, 8, 8, 512)
        frame[i] = y.transpose(1, 0, 2, 3).reshape(8, 32, 512).astype(BF)
        place = out_ref.at[pl.ds(8 * half, 8), pl.ds(32 * t, 32)]
        leave.append(pltpu.make_async_copy(frame.at[i], place, out_sem.at[i]))
        leave[-1].start()
    for copy in leave:
        copy.wait()


def body(features, conv_taps, block_gain, block_qkv, block_out, grid_gain, grid_qkv, grid_out):
    any_ = pl.BlockSpec(memory_space=pl.ANY)
    vmem = pl.BlockSpec(memory_space=pltpu.VMEM)
    dma = pltpu.SemaphoreType.DMA
    planes = (CHUNKS, PEERS, 32, 128)
    returned = pl.pallas_call(
        main_kernel,
        out_shape=pltpu.VMEM(planes, BF),
        in_specs=[any_] * 8,
        out_specs=vmem,
        scratch_shapes=[
            pltpu.VMEM((9, 512), F32),
            pltpu.VMEM((1, 512), F32),
            pltpu.VMEM((1, 512), F32),
            pltpu.VMEM((18, 96, 512), BF),
            pltpu.VMEM((16, 512), BF),
            pltpu.VMEM((16, 512), BF),
            pltpu.VMEM((3, 16, 512), BF),
            pltpu.VMEM((3, 16, 512), BF),
            pltpu.VMEM((3, 2, 4, 8, 8, 512), F32),
            pltpu.VMEM((2 * PEERS * 16, 128), F32),
            pltpu.VMEM((512, 1536), BF),
            pltpu.VMEM((512, 1536), BF),
            pltpu.VMEM((512, 512), BF),
            pltpu.VMEM((512, 512), BF),
            pltpu.VMEM((512, 512), BF),
            pltpu.VMEM((1024, 512), BF),
            pltpu.VMEM((2 * TOK, 512), BF),
            pltpu.VMEM((2, TOK, 512), BF),
            pltpu.VMEM((2 * TOK, 512), BF),
            pltpu.VMEM((1024, 2 * TOK), BF),
            pltpu.VMEM((512, 2 * TOK), BF),
            pltpu.VMEM(planes, BF),
            pltpu.VMEM(planes, BF),
            pltpu.VMEM(planes, BF),
            dma((10,)),
            dma((12,)),
            dma((12,)),
            dma((CHUNKS,)),
            dma((CHUNKS,)),
            dma((CHUNKS,)),
            dma((CHUNKS,)),
            dma((CHUNKS,)),
        ],
        compiler_params=pltpu.CompilerParams(
            collective_id=0, has_side_effects=True, vmem_limit_bytes=60 * 2**20
        ),
    )(
        features, conv_taps, block_gain.reshape(1, 512), grid_gain.reshape(1, 512),
        block_qkv, block_out, grid_qkv, grid_out,
    )
    return pl.pallas_call(
        unpack_kernel,
        out_shape=jax.ShapeDtypeStruct(features.shape, BF),
        in_specs=[vmem],
        out_specs=any_,
        scratch_shapes=[
            pltpu.VMEM((2 * CHUNKS, 8, 32, 512), BF),
            dma((2 * CHUNKS,)),
        ],
        compiler_params=pltpu.CompilerParams(vmem_limit_bytes=16 * 2**20),
    )(returned)


def solution(mesh):
    placed = (P("rows", "cols", None), P(), P(), P(), P(), P(), P(), P())
    return jax.shard_map(
        body, mesh=mesh, in_specs=placed, out_specs=P("rows", "cols", None), check_vma=False
    )
```
